256 devices in a mesh: dom: 32 (over x, z), feat: 8 (over y, core).
Axes of the slice: x: 4, y: 4, z: 8, core: 2. Of those that a mesh axis runs over, the one named last changes fastest.
Arguments:
- node_feats: bfloat16 [131072, 256], P(('dom', 'feat')), may hold values from -6 to 6
- w_query: bfloat16 [256, 256], replicated, may hold values from -0.375 to 0.375
- w_key: bfloat16 [256, 256], replicated, may hold values from -0.375 to 0.375
- w_value: bfloat16 [256, 256], replicated, may hold values from -0.375 to 0.375
- w_graph: bfloat16 [256, 256], replicated, may hold values from -0.375 to 0.375
- adj_tiles: bfloat16 [12288, 128, 128], P(('dom', 'feat')), may hold values from -0.15625 to 0.15625
- tile_rows: int32 [12288], P(('dom', 'feat')), may hold values from 0 to 4, as said below
- tile_cols: int32 [12288], P(('dom', 'feat')), may hold values from 0 to 47
- send_lists: int32 [32, 2, 8], P('dom'), may hold values from 0 to 31
- cotangent: bfloat16 [131072, 256], P(('dom', 'feat')), may hold values from -6 to 6
Outputs:
- layer_out: bfloat16 [131072, 256], P(('dom', 'feat'))
- grad_feats: bfloat16 [131072, 256], P(('dom', 'feat'))
- grad_query: float32 [256, 256], replicated
- grad_key: float32 [256, 256], replicated
- grad_value: float32 [256, 256], replicated
- grad_graph: float32 [256, 256], replicated
The draws below stay inside these ranges and needn't reach their ends.
Inputs may be any that keep to these rules, and one draw needn't show every extreme that they name: `tile_rows`: A slot holding 4 is empty; on each device the live slots come first, 12 to 48 of them, and some device has all 48 live. `send_lists`: blocks may repeat within a list.
All inputs are finite; a program needn't handle non-finite values.
Results may differ from the reference program's by a relative error of at most 0.0047.
The reference program's roundings to bfloat16 on the way count: a program that leaves them out, or rounds other values in their place, can miss the bound.
Values may be sent and summed in bfloat16 or wider, within the bound.
A program may use at most 128 MiB of HBM per device.

```python
import jax
import jax.numpy as jnp
from jax import lax

HEADS = 8
HEAD_DIM = 32
D = 256
BLK = 128
BLK_DEV = 4
TILES_DEV = 48
SEND = 8
PART_BLK = 32
EXT_BLK = 48
NODES = 131072
TILES = 12288
N_DOM = 32
N_FEAT = 8


def draw_tile_rows(key, part):
    key = jax.random.fold_in(key, 11)
    key_count, key_full, key_rows = jax.random.split(key, 3)
    device_count = TILES // TILES_DEV
    live_count = jax.random.randint(key_count, (device_count,), TILES_DEV // 4, TILES_DEV + 1)
    full_device = jax.random.randint(key_full, (), 0, device_count)
    live_count = jnp.where(jnp.arange(device_count) == full_device, TILES_DEV, live_count)
    row_blocks = jax.random.randint(key_rows, (device_count, TILES_DEV), 0, BLK_DEV)
    slot_index = jnp.arange(TILES_DEV)[None, :]
    row_blocks = jnp.where(slot_index < live_count[:, None], row_blocks, BLK_DEV)
    return row_blocks.reshape(TILES).astype(jnp.int32)


def plant(result, own_key, low, high):
    extent = result.shape
    place = [jax.random.randint(jax.random.fold_in(own_key, axis), (), 0, extent[axis]) for axis in range(len(extent))]
    result = result.at[tuple(place)].set(low)
    longest = extent.index(max(extent))
    place[longest] = (place[longest] + 1) % extent[longest]
    return result.at[tuple(place)].set(high)


def level_of(stream_key, extent, cuts, low, largest):
    gain = 1.0
    for dim, parts in cuts:
        draws = jax.random.uniform(jax.random.fold_in(jax.random.fold_in(stream_key, 6), dim), (parts,), jnp.float32, low / len(cuts), largest / len(cuts))
        gain = gain * jnp.repeat(jnp.exp(draws), extent[dim] // parts).reshape((-1,) + (1,) * (len(extent) - 1 - dim))
    return gain


def normal_values(stream_key, shape, spread, most, cuts=(), dtype=jnp.bfloat16):
    array = jax.random.normal(stream_key, shape, jnp.float32) * spread
    if len(cuts) > 0:
        array = level_of(stream_key, shape, cuts, -0.22, 0.18) * array
    return jnp.clip(array, min=-most, max=most).astype(dtype)


def setup_inputs(seed: int = 0) -> dict:
    arg_keys = jax.random.split(jax.random.key(seed), 11)
    return {
        "node_feats": normal_values(arg_keys[0], (NODES, D), 1.0, 6.0, ((0, 256),)),
        "w_query": normal_values(arg_keys[1], (D, D), D ** -0.5, 0.375),
        "w_key": normal_values(arg_keys[2], (D, D), D ** -0.5, 0.375),
        "w_value": normal_values(arg_keys[3], (D, D), D ** -0.5, 0.375),
        "w_graph": normal_values(arg_keys[4], (D, D), D ** -0.5, 0.375),
        "adj_tiles": normal_values(arg_keys[5], (TILES, BLK, BLK), (BLK * TILES_DEV // BLK_DEV) ** -0.5, 0.15625, ((0, 256),)),
        "tile_rows": draw_tile_rows(jax.random.fold_in(arg_keys[10], 71), 0),
        "tile_cols": plant(jax.random.randint(arg_keys[7], (TILES,), 0, EXT_BLK), jax.random.fold_in(arg_keys[7], 1), 0, EXT_BLK - 1).astype(jnp.int32),
        "send_lists": plant(jax.random.randint(arg_keys[8], (N_DOM, 2, SEND), 0, PART_BLK), jax.random.fold_in(arg_keys[8], 1), 0, PART_BLK - 1).astype(jnp.int32),
        "cotangent": normal_values(arg_keys[9], (NODES, D), 1.0, 6.0, ((0, 256),)),
    }


def feature_map(values):
    return jnp.where(values > 0, values + 1.0, jnp.exp(jnp.minimum(values, 0.0)))


def feature_slope(values):
    return jnp.where(values > 0, 1.0, jnp.exp(jnp.minimum(values, 0.0)))


def rounded(values):
    return lax.optimization_barrier(values.astype(jnp.bfloat16)).astype(jnp.float32)


def propagate(prop_in, adj_tiles, tile_rows, tile_cols, send_lists):
    precise = lax.Precision.HIGHEST
    part_blocks = prop_in.reshape(N_DOM, PART_BLK, BLK, D)
    pick = jax.vmap(lambda blocks, index_list: blocks[index_list])
    sent_lower = pick(part_blocks, send_lists[:, 0])
    sent_upper = pick(part_blocks, send_lists[:, 1])
    zero_rim = jnp.zeros((1, SEND, BLK, D), jnp.bfloat16)
    from_lower = jnp.concatenate([zero_rim, sent_upper[:-1]], 0)
    from_upper = jnp.concatenate([sent_lower[1:], zero_rim], 0)
    extended = jnp.concatenate([part_blocks, from_lower, from_upper], 1)
    device_count = N_DOM * N_FEAT
    tiles_dev = adj_tiles.reshape(device_count, TILES_DEV, BLK, BLK)
    rows_dev = tile_rows.reshape(device_count, TILES_DEV)
    cols_dev = tile_cols.reshape(device_count, TILES_DEV)
    owners = (jnp.arange(device_count) // N_FEAT).astype(jnp.int32)

    def one_device(inputs):
        tile_group, row_group, col_group, owner = inputs
        gathered = extended[owner][col_group].astype(jnp.float32)
        product = jnp.einsum('tij,tjd->tid', tile_group.astype(jnp.float32), gathered, precision=precise)
        onehot = (row_group[:, None] == jnp.arange(BLK_DEV)[None, :]).astype(jnp.float32)
        return jnp.einsum('tr,tid->rid', onehot, product, precision=precise)

    prop = lax.map(one_device, (tiles_dev, rows_dev, cols_dev, owners))
    return prop.reshape(NODES, D)


def propagate_back(grad_rows, adj_tiles, tile_rows, tile_cols, send_lists):
    precise = lax.Precision.HIGHEST
    part_grads = grad_rows.reshape(N_DOM, PART_BLK, BLK, D)
    padded = jnp.concatenate([part_grads, jnp.zeros((N_DOM, 1, BLK, D), jnp.bfloat16)], 1)
    tiles_part = adj_tiles.reshape(N_DOM, N_FEAT * TILES_DEV, BLK, BLK)
    rows_part = tile_rows.reshape(N_DOM, N_FEAT, TILES_DEV)
    offsets = (jnp.arange(N_FEAT) * BLK_DEV).astype(jnp.int32)[None, :, None]
    row_index = jnp.where(rows_part < BLK_DEV, rows_part + offsets, PART_BLK).astype(jnp.int32)
    row_index = row_index.reshape(N_DOM, N_FEAT * TILES_DEV)
    cols_part = tile_cols.reshape(N_DOM, N_FEAT * TILES_DEV)

    def one_part(inputs):
        padded_rows, tile_group, row_group, col_group = inputs
        taken = padded_rows[row_group].astype(jnp.float32)
        product = jnp.einsum('tij,tid->tjd', tile_group.astype(jnp.float32), taken, precision=precise)
        return jax.ops.segment_sum(product, col_group, num_segments=EXT_BLK)

    ext_grads = lax.map(one_part, (padded, tiles_part, row_index, cols_part))
    own = ext_grads[:, :PART_BLK]
    lower_rims = ext_grads[:, PART_BLK:PART_BLK + SEND]
    upper_rims = ext_grads[:, PART_BLK + SEND:]
    zero_rim = jnp.zeros((1, SEND, BLK, D), jnp.float32)
    from_above = jnp.concatenate([lower_rims[1:], zero_rim], 0)
    from_below = jnp.concatenate([zero_rim, upper_rims[:-1]], 0)
    add_rows = jax.vmap(lambda base_rows, index_list, values: base_rows.at[index_list].add(values))
    own = add_rows(own, send_lists[:, 1], from_above)
    own = add_rows(own, send_lists[:, 0], from_below)
    return own.reshape(NODES, D)


def reference(node_feats, w_query, w_key, w_value, w_graph, adj_tiles, tile_rows, tile_cols, send_lists, cotangent):
    precise = lax.Precision.HIGHEST
    query_proj = jnp.dot(node_feats, w_query, preferred_element_type=jnp.float32)
    key_proj = jnp.dot(node_feats, w_key, preferred_element_type=jnp.float32)
    value_proj = jnp.dot(node_feats, w_value, preferred_element_type=jnp.float32)
    graph_proj = jnp.dot(node_feats, w_graph, preferred_element_type=jnp.float32)
    shape_heads = (NODES, HEADS, HEAD_DIM)
    q_heads = rounded(feature_map(query_proj)).reshape(shape_heads)
    k_heads = rounded(feature_map(key_proj)).reshape(shape_heads)
    v_heads = rounded(value_proj).reshape(shape_heads)
    prop_in = graph_proj.astype(jnp.bfloat16)
    kv_state = jnp.einsum('nhi,nhj->hij', k_heads, v_heads, precision=precise)
    key_sum = jnp.sum(k_heads, axis=0)
    numerator = jnp.einsum('nhi,hij->nhj', q_heads, kv_state, precision=precise)
    denominator = jnp.einsum('nhi,hi->nh', q_heads, key_sum, precision=precise)
    attn = numerator / denominator[:, :, None]
    prop = propagate(prop_in, adj_tiles, tile_rows, tile_cols, send_lists)
    layer_out = (0.5 * attn.reshape(NODES, D) + 0.5 * prop).astype(jnp.bfloat16)

    grad_half = cotangent.astype(jnp.float32) * 0.5
    grad_heads = grad_half.reshape(shape_heads)
    d_numer = grad_heads / denominator[:, :, None]
    d_denom = -jnp.sum(grad_heads * attn, axis=-1) / denominator
    d_qfeat = jnp.einsum('nhj,hij->nhi', d_numer, kv_state, precision=precise) + d_denom[:, :, None] * key_sum[None]
    d_state = jnp.einsum('nhi,nhj->hij', q_heads, d_numer, precision=precise)
    d_keysum = jnp.einsum('nh,nhi->hi', d_denom, q_heads, precision=precise)
    d_kfeat = jnp.einsum('nhj,hij->nhi', v_heads, d_state, precision=precise) + d_keysum[None]
    d_value = jnp.einsum('nhi,hij->nhj', k_heads, d_state, precision=precise).reshape(NODES, D)
    d_query = d_qfeat.reshape(NODES, D) * feature_slope(query_proj)
    d_key = d_kfeat.reshape(NODES, D) * feature_slope(key_proj)
    prop_grad = propagate_back(grad_half.astype(jnp.bfloat16), adj_tiles, tile_rows, tile_cols, send_lists)

    grad_feats = jnp.dot(d_query, w_query.astype(jnp.float32).T, precision=precise)
    grad_feats = grad_feats + jnp.dot(d_key, w_key.astype(jnp.float32).T, precision=precise)
    grad_feats = grad_feats + jnp.dot(d_value, w_value.astype(jnp.float32).T, precision=precise)
    grad_feats = grad_feats + jnp.dot(prop_grad, w_graph.astype(jnp.float32).T, precision=precise)
    feats_wide = node_feats.astype(jnp.float32)
    grad_query = jnp.dot(feats_wide.T, d_query, precision=precise)
    grad_key = jnp.dot(feats_wide.T, d_key, precision=precise)
    grad_value = jnp.dot(feats_wide.T, d_value, precision=precise)
    grad_graph = jnp.dot(feats_wide.T, prop_grad, precision=precise)
    return (layer_out, grad_feats.astype(jnp.bfloat16), grad_query, grad_key, grad_value, grad_graph)
```

```python
import functools

import jax
import jax.numpy as jnp
from jax import lax
from jax.experimental import pallas as pl
from jax.experimental.pallas import tpu as pltpu
from jax.sharding import PartitionSpec as P

HEADS = 8
HD = 32
MESH = pl.DeviceIdType.MESH
F32 = jnp.float32
BF16 = jnp.bfloat16
CORES = 2
LIMIT = 56 * 1024 * 1024

VM = pl.BlockSpec(memory_space=pltpu.VMEM)
SM = pl.BlockSpec(memory_space=pltpu.SMEM)
HB = pl.BlockSpec(memory_space=pl.ANY)


def dims(mesh_dom):
    zn = min(8, mesh_dom)
    return mesh_dom // zn, zn


def dot(a, b):
    return jnp.dot(a, b, preferred_element_type=F32)


def dot_tn(a, b):
    return lax.dot_general(a, b, (((0,), (0,)), ((), ())), preferred_element_type=F32)


def dot_nt(a, b):
    return lax.dot_general(a, b, (((1,), (1,)), ((), ())), preferred_element_type=F32)


def split(value, parts):
    out = []
    for _ in range(parts - 1):
        top = value.astype(BF16)
        out.append(top)
        value = value - top.astype(F32)
    out.append(value.astype(BF16))
    return out


def dots(op, a, b):
    terms = [op(p, q) for p in a for q in b]
    total = terms[-1]
    for term in terms[-2::-1]:
        total = total + term
    return total


def feature(z):
    return jnp.where(z > 0, z + 1.0, jnp.exp(jnp.minimum(z, 0.0)))


def slope(z):
    return jnp.where(z > 0, 1.0, jnp.exp(jnp.minimum(z, 0.0)))


def same_head(rows, cols):
    r = lax.broadcasted_iota(jnp.int32, (rows, cols), 0) // HD
    c = lax.broadcasted_iota(jnp.int32, (rows, cols), 1) // HD
    return r == c


def compact(full):
    lane = lax.broadcasted_iota(jnp.int32, (HD, full.shape[1]), 1) // HD
    out = jnp.zeros((HD, full.shape[1]), F32)
    for h in range(HEADS):
        out = out + jnp.where(lane == h, full[h * HD : (h + 1) * HD, :], 0.0)
    return out


def block_diag(small):
    width = small.shape[1]
    return jnp.where(same_head(width, width), jnp.concatenate([small] * HEADS, 0), 0.0)


def state_store(st_ref, small, row):
    for s in range(4):
        st_ref[s] = small[8 * s : 8 * s + 8]
    st_ref[4] = jnp.broadcast_to(row, (8, row.shape[1]))
    for s in range(5, 8):
        st_ref[s] = jnp.zeros((8, row.shape[1]), F32)


def state_load(st_ref):
    small = jnp.concatenate([st_ref[s] for s in range(4)], 0)
    return small, st_ref[4][0:1]


def first_kernel(
    rows, cols, x, wq, wk, wv, wg, adj, cot, qf, kf, vf, pin, st, pext, acc, g5
):
    tiles = adj.shape[0]
    blocks, size = g5.shape[0] - 1, g5.shape[1]
    xv = x[...]
    k = feature(dot(xv, wk[...])).astype(BF16)
    v = dot(xv, wv[...]).astype(BF16)
    kf[...] = k
    vf[...] = v
    state_store(st, compact(dot_tn(k, v)), jnp.sum(k.astype(F32), axis=0, keepdims=True))
    qf[...] = feature(dot(xv, wq[...])).astype(BF16)
    pin[...] = dot(xv, wg[...]).astype(BF16).reshape(pin.shape)
    for b in range(blocks):
        g5[b] = (cot[b * size : (b + 1) * size, :].astype(F32) * 0.5).astype(BF16)
    g5[blocks] = jnp.zeros(g5.shape[1:], BF16)

    def clear(c, carry):
        acc[c] = jnp.zeros(acc.shape[1:], F32)
        return carry

    lax.fori_loop(0, acc.shape[0], clear, 0)

    def one(t, carry):
        product = dot_tn(adj[t], g5[rows[t]])
        c = cols[t]
        acc[c] = acc[c] + product
        return carry

    lax.fori_loop(0, tiles, one, 0, unroll=4)

    def low(c, carry):
        pext[c] = acc[c].astype(BF16)
        return carry

    lax.fori_loop(0, acc.shape[0], low, 0)


def place(zn):
    d, f = lax.axis_index("dom"), lax.axis_index("feat")
    return d, f, d // zn, d % zn, f // CORES, f % CORES


def greet(peers):
    barrier = pltpu.get_barrier_semaphore()
    for peer in peers:
        pl.semaphore_signal(barrier, inc=1, device_id=peer, device_id_type=MESH)
    pl.semaphore_wait(barrier, len(peers))


def send(src, dst, ssem, rsem, dev):
    copy = pltpu.make_async_remote_copy(
        src_ref=src, dst_ref=dst, send_sem=ssem, recv_sem=rsem, device_id=dev, device_id_type=MESH
    )
    copy.start()
    return copy


def ring_peers(xn, zn, yn):
    d, f, x, z, y, c = place(zn)
    feat = [(d, (f + k) % (yn * CORES)) for k in range(1, yn * CORES)]
    zs = [(x * zn + (z + k) % zn, f) for k in range(1, zn)]
    xs = [((x + k) % xn * zn + z, f) for k in range(1, xn)]
    return feat, zs, xs


class Reduce:
    def __init__(self, xn, zn, yn, st, out, rsbuf, zbuf, xbuf, ssem, rsem):
        self.xn, self.zn, self.yn = xn, zn, yn
        self.st, self.out, self.rsbuf, self.zbuf, self.xbuf = st, out, rsbuf, zbuf, xbuf
        self.ssem, self.rsem = ssem, rsem
        self.used = 0
        self.sent = []
        self.d, self.f, self.x, self.z, self.y, self.c = place(zn)
        self.feat, self.zs, self.xs = ring_peers(xn, zn, yn)

    def spread(self, srcs, dst, peers):
        copies = []
        for src, peer in zip(srcs, peers):
            n = self.used
            self.used += 1
            copies.append(send(src, dst, self.ssem.at[n], self.rsem.at[n], peer))
        self.sent += copies
        return copies

    def scatter(self):
        n = len(self.feat) + 1
        self.pending = self.spread(
            [self.st.at[(self.f + k) % n] for k in range(1, n)], self.rsbuf.at[self.f], self.feat
        )
        self.rsbuf[self.f] = self.st[self.f]

    def total(self, buf):
        for copy in self.pending:
            copy.wait_recv()
        value = buf[0]
        for i in range(1, buf.shape[0]):
            value = value + buf[i]
        return value

    def along_z(self):
        self.zbuf[self.z] = self.total(self.rsbuf)
        self.pending = self.spread([self.zbuf.at[self.z]] * len(self.zs), self.zbuf.at[self.z], self.zs)

    def along_x(self):
        self.xbuf[self.x] = self.total(self.zbuf)
        self.pending = self.spread([self.xbuf.at[self.x]] * len(self.xs), self.xbuf.at[self.x], self.xs)

    def gather(self):
        self.out[self.f] = self.total(self.xbuf)
        self.pending = self.spread([self.out.at[self.f]] * len(self.feat), self.out.at[self.f], self.feat)

    def finish(self):
        for copy in self.pending:
            copy.wait_recv()
        for copy in self.sent:
            copy.wait_send()


def reduce_scratch(xn, zn, yn, width):
    count = 2 * (yn * CORES - 1) + zn - 1 + xn - 1
    return [
        pltpu.VMEM((8, 8, width), F32),
        pltpu.VMEM((zn, 8, width), F32),
        pltpu.VMEM((xn, 8, width), F32),
        pltpu.SemaphoreType.DMA((count,)),
        pltpu.SemaphoreType.DMA((count,)),
    ]


def second_kernel(
    xn, zn, yn,
    st, pin, pext,
    out, part, own, back,
    rsbuf, zbuf, xbuf, rs_s, rs_r,
    sib, rimsum, ag_s, ag_r, rb_s, rb_r,
):
    d, f, x, z, y, c = place(zn)
    dn = xn * zn
    feat, zs, xs = ring_peers(xn, zn, yn)
    sibling = (d, f + 1 - 2 * c)
    up_y = (d, (y + 1) % yn * CORES + c)
    down_y = (d, (y + yn - 1) % yn * CORES + c)
    above, below = ((d + 1) % dn, f), ((d + dn - 1) % dn, f)
    mine = pin.shape[0]
    half = mine // 2
    hrow = sib.shape[1]
    nown = own.shape[0]
    nrim = sib.shape[0] - nown
    greet(feat + zs + xs + [above, below])

    red = Reduce(xn, zn, yn, st, out, rsbuf, zbuf, xbuf, rs_s, rs_r)
    red.scatter()
    other = pl.ds(pl.multiple_of(hrow * (1 - c), hrow), hrow)
    keep = pl.ds(pl.multiple_of(hrow * c, hrow), hrow)
    sib_rim = send(
        pext.at[pl.ds(nown, nrim), other], sib.at[pl.ds(nown, nrim)], rb_s.at[0], rb_r.at[0], sibling
    )

    def chunk(dev_f, h, count=1):
        return part.at[pl.ds(dev_f * mine + h * half, half * count)]

    part[pl.ds(f * mine, mine)] = pin[...]
    a0 = send(chunk(f, 0), chunk(f, 0), ag_s.at[0], ag_r.at[0], up_y)
    b1 = send(chunk(f, 1), chunk(f, 1), ag_s.at[1], ag_r.at[1], down_y)
    a1 = send(chunk(f, 1), chunk(f, 1), ag_s.at[2], ag_r.at[2], up_y)
    b0 = send(chunk(f, 0), chunk(f, 0), ag_s.at[3], ag_r.at[3], down_y)
    s_own = send(chunk(f, 0, 2), chunk(f, 0, 2), ag_s.at[4], ag_r.at[4], sibling)
    sib_own = send(
        pext.at[pl.ds(0, nown), other], sib.at[pl.ds(0, nown)], rb_s.at[1], rb_r.at[1], sibling
    )

    red.along_z()

    sib_rim.wait_recv()

    def add_rim(i, carry):
        rimsum[i] = (pext[nown + i, keep].astype(F32) + sib[nown + i].astype(F32)).astype(BF16)
        return carry

    lax.fori_loop(0, nrim, add_rim, 0)
    nb = nrim // 2
    to_below = send(rimsum.at[pl.ds(0, nb)], back.at[0], rb_s.at[2], rb_r.at[2], below)
    to_above = send(rimsum.at[pl.ds(nb, nb)], back.at[1], rb_s.at[3], rb_r.at[3], above)

    fu = (y + 1) % yn * CORES + c
    fd = (y + yn - 1) % yn * CORES + c
    fo = (y + 2) % yn * CORES + c
    a0.wait_recv()
    fa = send(chunk(fd, 0), chunk(fd, 0), ag_s.at[5], ag_r.at[5], up_y)
    s0 = send(chunk(fd, 0), chunk(fd, 0), ag_s.at[7], ag_r.at[7], sibling)
    b1.wait_recv()
    fb = send(chunk(fu, 1), chunk(fu, 1), ag_s.at[6], ag_r.at[6], down_y)
    s1 = send(chunk(fu, 1), chunk(fu, 1), ag_s.at[8], ag_r.at[8], sibling)
    red.along_x()
    red.gather()

    sib_own.wait_recv()

    def add_own(i, carry):
        own[i] = pext[i, keep].astype(F32) + sib[i].astype(F32)
        return carry

    lax.fori_loop(0, nown, add_own, 0)

    a1.wait_recv()
    s2 = send(chunk(fd, 1), chunk(fd, 1), ag_s.at[9], ag_r.at[9], sibling)
    b0.wait_recv()
    s3 = send(chunk(fu, 0), chunk(fu, 0), ag_s.at[10], ag_r.at[10], sibling)
    fa.wait_recv()
    s4 = send(chunk(fo, 0), chunk(fo, 0), ag_s.at[11], ag_r.at[11], sibling)
    fb.wait_recv()
    s5 = send(chunk(fo, 1), chunk(fo, 1), ag_s.at[12], ag_r.at[12], sibling)
    for copy in (to_below, to_above, s_own, s0, s1, s2, s3, s4, s5):
        copy.wait_recv()

    @pl.when(d == dn - 1)
    def _():
        back[0] = jnp.zeros(back.shape[1:], BF16)

    @pl.when(d == 0)
    def _():
        back[1] = jnp.zeros(back.shape[1:], BF16)

    red.finish()
    for copy in (sib_rim, sib_own, to_below, to_above, a0, b1, a1, b0, s_own, fa, fb, s0, s1, s2, s3, s4, s5):
        copy.wait_send()


def third_kernel(lists, st, qf, cot, x, wq, part, own, back, attn_o, dq_o, st2, own_o, picks, work):
    small, ks = state_load(st)
    width = ks.shape[1]
    kv = split(block_diag(small), 3)
    ks_col = jnp.broadcast_to(ks, (128, width)).T
    head = same_head(width, width)
    ks_bd = split(jnp.where(head, jnp.concatenate([ks_col] * (width // 128), 1), 0.0), 3)
    q = qf[...]
    den = dots(dot, [q], ks_bd)
    rden = 1.0 / den
    attn = dots(dot, [q], kv) * rden
    attn_o[...] = attn
    g = cot[...].astype(F32) * 0.5
    ones = jnp.where(head, 1.0, 0.0).astype(BF16)
    dden = -dots(dot, split(g * attn, 3), [ones]) * rden
    dqf = dots(dot_nt, [g.astype(BF16)], kv) * rden + dden * ks
    dq_o[...] = dqf * slope(dot(x[...], wq[...]))
    dstate = compact(dots(dot_tn, [q], split(g * rden, 3)))
    state_store(st2, dstate, jnp.sum(dden * q.astype(F32), axis=0, keepdims=True))

    nb = lists.shape[1]
    for i in range(own.shape[0]):
        work[i] = own[i]
    for s in range(nb):
        up, down = lists[1, s], lists[0, s]
        work[up] = work[up] + back[0, s].astype(F32)
        work[down] = work[down] + back[1, s].astype(F32)
        picks[0, s] = part[up]
        picks[1, s] = part[down]
    for i in range(own.shape[0]):
        own_o[i] = work[i].astype(BF16)


def fourth_kernel(
    xn, zn, yn,
    st, own, picks,
    out, rim, pg,
    rsbuf, zbuf, xbuf, rs_s, rs_r,
    ybuf, ysum, res, y_s, y_r, f_s, f_r,
):
    d, f, x, z, y, c = place(zn)
    dn = xn * zn
    feat, zs, xs = ring_peers(xn, zn, yn)
    sibling = (d, f + 1 - 2 * c)
    yu, yd, yo = (y + 1) % yn, (y + yn - 1) % yn, (y + 2) % yn
    up_y, down_y = (d, yu * CORES + c), (d, yd * CORES + c)
    above, below = ((d + 1) % dn, f), ((d + dn - 1) % dn, f)
    per = own.shape[0] // yn
    hb = per // 2
    hrow = own.shape[1]
    greet(feat + zs + xs + [above, below])

    red = Reduce(xn, zn, yn, st, out, rsbuf, zbuf, xbuf, rs_s, rs_r)
    red.scatter()

    def piece(yy, h):
        return own.at[pl.ds(yy * per + h * hb, hb)]

    keep = pl.ds(pl.multiple_of(hrow * c, hrow), hrow)
    y0 = send(piece(yo, 0), ybuf.at[0], y_s.at[0], y_r.at[0], up_y)
    y1 = send(piece(yo, 1), ybuf.at[1], y_s.at[1], y_r.at[1], down_y)
    y2 = send(piece(yu, 1), ybuf.at[2], y_s.at[2], y_r.at[2], up_y)
    y3 = send(piece(yd, 0), ybuf.at[3], y_s.at[3], y_r.at[3], down_y)
    to_above = send(picks.at[0, :, keep], rim.at[0, :, keep], f_s.at[0], f_r.at[0], above)
    to_below = send(picks.at[1, :, keep], rim.at[1, :, keep], f_s.at[1], f_r.at[1], below)

    red.along_z()

    y0.wait_recv()

    def add0(i, carry):
        ysum[0, i] = (own[yu * per + i].astype(F32) + ybuf[0, i].astype(F32)).astype(BF16)
        return carry

    lax.fori_loop(0, hb, add0, 0)
    y4 = send(ysum.at[0], ybuf.at[4], y_s.at[4], y_r.at[4], up_y)
    y1.wait_recv()

    def add1(i, carry):
        ysum[1, i] = (own[yd * per + hb + i].astype(F32) + ybuf[1, i].astype(F32)).astype(BF16)
        return carry

    lax.fori_loop(0, hb, add1, 0)
    y5 = send(ysum.at[1], ybuf.at[5], y_s.at[5], y_r.at[5], down_y)
    red.along_x()
    red.gather()

    to_above.wait_recv()
    s0 = send(rim.at[0, :, keep], rim.at[0, :, keep], f_s.at[2], f_r.at[2], sibling)
    to_below.wait_recv()
    s1 = send(rim.at[1, :, keep], rim.at[1, :, keep], f_s.at[3], f_r.at[3], sibling)

    for copy in (y2, y3, y4, y5):
        copy.wait_recv()

    def last(i, carry):
        base = y * per
        res[i] = own[base + i].astype(F32) + ybuf[4, i].astype(F32) + ybuf[3, i].astype(F32)
        res[hb + i] = own[base + hb + i].astype(F32) + ybuf[2, i].astype(F32) + ybuf[5, i].astype(F32)
        return carry

    lax.fori_loop(0, hb, last, 0)
    pg_copy = send(res.at[pl.ds(hb * (1 - c), hb)], pg.at[:, keep], y_s.at[6], y_r.at[6], sibling)
    pg[:, keep] = res[pl.ds(hb * c, hb)]
    pg_copy.wait_recv()
    s0.wait_recv()
    s1.wait_recv()
    for copy in (s0, s1, pg_copy, to_above, to_below, y0, y1, y2, y3, y4, y5):
        copy.wait_send()

    @pl.when(d == 0)
    def _():
        rim[0] = jnp.zeros(rim.shape[1:], BF16)

    @pl.when(d == dn - 1)
    def _():
        rim[1] = jnp.zeros(rim.shape[1:], BF16)

    red.finish()


def fifth_kernel(
    rows, cols, x, wq, wk, wv, wg, kf, vf, attn, dq, st, part, rim, adj, pg,
    layer, gfeat, local,
    ext, acc, sems,
):
    nown = part.shape[0]
    nb = rim.shape[1]
    copies = [
        pltpu.make_async_copy(part, ext.at[pl.ds(0, nown)], sems.at[0]),
        pltpu.make_async_copy(rim.at[0], ext.at[pl.ds(nown, nb)], sems.at[1]),
        pltpu.make_async_copy(rim.at[1], ext.at[pl.ds(nown + nb, nb)], sems.at[2]),
    ]
    for copy in copies:
        copy.start()
    small, dks = state_load(st)
    ds = split(block_diag(small), 2)
    xv = x[...]
    v = vf[...]
    dk = (dots(dot_nt, [v], ds) + dks) * slope(dot(xv, wk[...]))
    dv = dots(dot, [kf[...]], ds)
    pgv = pg[...].reshape(xv.shape)
    total = None
    for i, (grad, w) in enumerate(((dq[...], wq), (dk, wk), (dv, wv), (pgv, wg))):
        parts = split(grad, 2)
        local[i] = dots(dot_tn, [xv], parts)
        term = dots(dot_nt, parts, [w[...]])
        total = term if total is None else total + term
    gfeat[...] = total.astype(BF16)
    for copy in copies:
        copy.wait()
    acc[...] = jnp.zeros(acc.shape, F32)

    def one(t, carry):
        r = rows[t]
        acc[r] = acc[r] + dot(adj[t], ext[cols[t]])
        return carry

    lax.fori_loop(0, adj.shape[0], one, 0, unroll=4)
    size = acc.shape[1]
    for b in range(acc.shape[0] - 1):
        here = slice(b * size, (b + 1) * size)
        layer[here, :] = (0.5 * attn[here, :] + 0.5 * acc[b]).astype(BF16)


def sixth_kernel(xn, zn, yn, local, out, sbuf, ybuf, h1, h2, xbuf, h3, zbuf, s_s, s_r):
    d, f, x, z, y, c = place(zn)
    sibling = (d, f + 1 - 2 * c)
    ys = [(d, (y + k) % yn * CORES + c) for k in range(1, yn)]
    _, zs, xs = ring_peers(xn, zn, yn)
    greet([sibling] + ys + zs + xs)
    nm = local.shape[0]
    hrow = sbuf.shape[1]
    yrow = hrow // yn
    xrow = yrow // xn
    used = [0]
    sent = []

    def go(src, dst, dev):
        n = used[0]
        used[0] += 1
        copy = send(src, dst, s_s.at[n], s_r.at[n], dev)
        sent.append(copy)
        return copy

    def rows_of(start, count):
        return pl.ds(pl.multiple_of(start, count), count)

    first = go(local.at[:, rows_of(hrow * (1 - c), hrow)], sbuf, sibling)
    first.wait_recv()

    def add1(m, carry):
        h1[m] = local[m, rows_of(hrow * c, hrow)] + sbuf[m]
        return carry

    lax.fori_loop(0, nm, add1, 0)
    copies = [
        go(h1.at[:, rows_of((y + k) % yn * yrow, yrow)], ybuf.at[k - 1], ys[k - 1]) for k in range(1, yn)
    ]
    for copy in copies:
        copy.wait_recv()

    def add2(m, carry):
        value = h1[m, rows_of(y * yrow, yrow)]
        for k in range(1, yn):
            value = value + ybuf[k - 1, m]
        h2[m] = value
        return carry

    lax.fori_loop(0, nm, add2, 0)
    copies = [
        go(h2.at[:, rows_of((x + k) % xn * xrow, xrow)], xbuf.at[k - 1], xs[k - 1]) for k in range(1, xn)
    ]
    for copy in copies:
        copy.wait_recv()
    lanes = h2.shape[2] // 128
    units = h3.shape[0]
    for m in range(nm):
        value = h2[m, rows_of(x * xrow, xrow)]
        for k in range(1, xn):
            value = value + xbuf[k - 1, m]
        for r in range(xrow // 8):
            for a in range(lanes):
                h3[(m * (xrow // 8) + r) * lanes + a] = value[r * 8 : r * 8 + 8, a * 128 : a * 128 + 128]
    uz = units // zn
    copies = [
        go(h3.at[pl.ds((z + k) % zn * uz, uz)], zbuf.at[k - 1], zs[k - 1]) for k in range(1, zn)
    ]
    for copy in copies:
        copy.wait_recv()
    value = h3[pl.ds(z * uz, uz)]
    for k in range(1, zn):
        value = value + zbuf[k - 1]
    here = out.at[c, y, x, pl.ds(z * uz, uz)]
    out[c, y, x, pl.ds(z * uz, uz)] = value
    for copy in [go(here, here, peer) for peer in zs]:
        copy.wait_recv()
    for copy in [go(out.at[c, y, x], out.at[c, y, x], peer) for peer in xs]:
        copy.wait_recv()
    for copy in [go(out.at[c, y], out.at[c, y], peer) for peer in ys]:
        copy.wait_recv()
    go(out.at[c], out.at[c], sibling).wait_recv()
    for copy in sent:
        copy.wait_send()


def seventh_kernel(out, g0, g1, g2, g3):
    cn, yn, xn, units = out.shape[:4]
    grads = (g0, g1, g2, g3)
    lanes = g0.shape[1] // 128
    per = units // len(grads) // lanes
    for c in range(cn):
        for y in range(yn):
            for x in range(xn):
                for m, ref in enumerate(grads):
                    for r in range(per):
                        row = (((c * yn + y) * xn + x) * per + r) * 8
                        for a in range(lanes):
                            ref[row : row + 8, a * 128 : a * 128 + 128] = out[c, y, x, (m * per + r) * lanes + a]


def plain(limit=LIMIT):
    return pltpu.CompilerParams(vmem_limit_bytes=limit)


def linked(number, limit=LIMIT):
    return pltpu.CompilerParams(collective_id=number, has_side_effects=True, vmem_limit_bytes=limit)


def shards(xn, zn, x, wq, wk, wv, wg, adj, rows, cols, lists, cot):
    yn = lax.axis_size("feat") // CORES
    n, w = x.shape
    tiles, size = adj.shape[0], adj.shape[1]
    local_blocks = n // size
    nown = local_blocks * yn * CORES
    nb = lists.shape[2]
    next_ = nown + 2 * nb
    lists = lists.reshape(lists.shape[1:])
    S = jax.ShapeDtypeStruct
    half = size // 2

    qf, kf, vf, pin, st, pext = pl.pallas_call(
        first_kernel,
        out_shape=[
            S((n, w), BF16), S((n, w), BF16), S((n, w), BF16), S((local_blocks, size, w), BF16),
            S((8, 8, w), F32), S((next_, size, w), BF16),
        ],
        in_specs=[SM, SM] + [VM] * 7,
        out_specs=[VM] * 6,
        scratch_shapes=[pltpu.VMEM((next_, size, w), F32), pltpu.VMEM((local_blocks + 1, size, w), BF16)],
        compiler_params=plain(),
        name="first",
    )(rows, cols, x, wq, wk, wv, wg, adj, cot)

    st, part, own, back = pl.pallas_call(
        functools.partial(second_kernel, xn, zn, yn),
        out_shape=[
            S((8, 8, w), F32), S((nown, size, w), BF16), S((nown, half, w), F32), S((2, nb, half, w), BF16),
        ],
        in_specs=[VM] * 3,
        out_specs=[VM] * 4,
        scratch_shapes=reduce_scratch(xn, zn, yn, w) + [
            pltpu.VMEM((next_, half, w), BF16),
            pltpu.VMEM((2 * nb, half, w), BF16),
            pltpu.SemaphoreType.DMA((13,)),
            pltpu.SemaphoreType.DMA((13,)),
            pltpu.SemaphoreType.DMA((4,)),
            pltpu.SemaphoreType.DMA((4,)),
        ],
        compiler_params=linked(0),
        name="second",
    )(st, pin, pext)

    attn, dq, st2, own, picks = pl.pallas_call(
        third_kernel,
        out_shape=[
            S((n, w), F32), S((n, w), F32), S((8, 8, w), F32), S((nown, half, w), BF16),
            S((2, nb, size, w), BF16),
        ],
        in_specs=[SM] + [VM] * 8,
        out_specs=[VM] * 5,
        scratch_shapes=[pltpu.VMEM((nown, half, w), F32)],
        compiler_params=plain(),
        name="third",
    )(lists, st, qf, cot, x, wq, part, own, back)

    st2, rim, pg = pl.pallas_call(
        functools.partial(fourth_kernel, xn, zn, yn),
        out_shape=[S((8, 8, w), F32), S((2, nb, size, w), BF16), S((local_blocks, size, w), F32)],
        in_specs=[VM] * 3,
        out_specs=[VM] * 3,
        scratch_shapes=reduce_scratch(xn, zn, yn, w) + [
            pltpu.VMEM((6, local_blocks, half, w), BF16),
            pltpu.VMEM((2, local_blocks, half, w), BF16),
            pltpu.VMEM((2 * local_blocks, half, w), F32),
            pltpu.SemaphoreType.DMA((7,)),
            pltpu.SemaphoreType.DMA((7,)),
            pltpu.SemaphoreType.DMA((4,)),
            pltpu.SemaphoreType.DMA((4,)),
        ],
        compiler_params=linked(1),
        name="fourth",
    )(st2, own, picks)

    layer, gfeat, local = pl.pallas_call(
        fifth_kernel,
        out_shape=[S((n, w), BF16), S((n, w), BF16), S((4, w, w), F32)],
        in_specs=[SM, SM] + [VM] * 10 + [HB, HB] + [VM] * 2,
        out_specs=[VM] * 3,
        scratch_shapes=[
            pltpu.VMEM((next_, size, w), BF16),
            pltpu.VMEM((local_blocks + 1, size, w), F32),
            pltpu.SemaphoreType.DMA((3,)),
        ],
        compiler_params=plain(),
        name="fifth",
    )(rows, cols, x, wq, wk, wv, wg, kf, vf, attn, dq, st2, part, rim, adj, pg)

    yrow = w // CORES // yn
    xrow = yrow // xn
    units = 4 * (xrow // 8) * (w // 128)
    count = 2 * (1 + yn - 1 + xn - 1 + zn - 1)
    out = pl.pallas_call(
        functools.partial(sixth_kernel, xn, zn, yn),
        out_shape=S((CORES, yn, xn, units, 8, 128), F32),
        in_specs=[VM],
        out_specs=VM,
        scratch_shapes=[
            pltpu.VMEM((4, w // CORES, w), F32),
            pltpu.VMEM((yn - 1, 4, yrow, w), F32),
            pltpu.VMEM((4, w // CORES, w), F32),
            pltpu.VMEM((4, yrow, w), F32),
            pltpu.VMEM((max(xn - 1, 1), 4, xrow, w), F32),
            pltpu.VMEM((units, 8, 128), F32),
            pltpu.VMEM((max(zn - 1, 1), units // zn, 8, 128), F32),
            pltpu.SemaphoreType.DMA((count,)),
            pltpu.SemaphoreType.DMA((count,)),
        ],
        compiler_params=linked(2),
        name="sixth",
    )(local)

    grads = pl.pallas_call(
        seventh_kernel,
        out_shape=[S((w, w), F32)] * 4,
        in_specs=[VM],
        out_specs=[VM] * 4,
        compiler_params=plain(),
        name="seventh",
    )(out)
    return (layer, gfeat, *grads)


def solution(mesh):
    xn, zn = dims(mesh.shape["dom"])
    return jax.shard_map(
        functools.partial(shards, xn, zn),
        mesh=mesh,
        in_specs=(
            P(("dom", "feat"), None),
            P(),
            P(),
            P(),
            P(),
            P(("dom", "feat"), None, None),
            P(("dom", "feat")),
            P(("dom", "feat")),
            P("dom", None, None),
            P(("dom", "feat"), None),
        ),
        out_specs=(P(("dom", "feat"), None), P(("dom", "feat"), None), P(), P(), P(), P()),
        check_vma=False,
    )
```

```python
import functools
from types import SimpleNamespace

import jax
import jax.numpy as jnp
from jax import lax
from jax.experimental import pallas as pl
from jax.experimental.pallas import tpu as pltpu
from jax.sharding import PartitionSpec as P

HEADS = 8
HD = 32
MESH = pl.DeviceIdType.MESH
F32 = jnp.float32
BF16 = jnp.bfloat16
CORES = 2
LIMIT = 56 * 1024 * 1024

VM = pl.BlockSpec(memory_space=pltpu.VMEM)
SM = pl.BlockSpec(memory_space=pltpu.SMEM)
HB = pl.BlockSpec(memory_space=pl.ANY)


def dims(mesh_dom):
    zn = min(8, mesh_dom)
    return mesh_dom // zn, zn


def dot(a, b):
    return jnp.dot(a, b, preferred_element_type=F32)


def dot_tn(a, b):
    return lax.dot_general(a, b, (((0,), (0,)), ((), ())), preferred_element_type=F32)


def dot_nt(a, b):
    return lax.dot_general(a, b, (((1,), (1,)), ((), ())), preferred_element_type=F32)


def split(value, parts):
    out = []
    for _ in range(parts - 1):
        top = value.astype(BF16)
        out.append(top)
        value = value - top.astype(F32)
    out.append(value.astype(BF16))
    return out


def dots(op, a, b):
    terms = [op(p, q) for p in a for q in b]
    total = terms[-1]
    for term in terms[-2::-1]:
        total = total + term
    return total


def feature(z):
    return jnp.where(z > 0, z + 1.0, jnp.exp(jnp.minimum(z, 0.0)))


def slope(z):
    return jnp.where(z > 0, 1.0, jnp.exp(jnp.minimum(z, 0.0)))


def same_head(rows, cols):
    r = lax.broadcasted_iota(jnp.int32, (rows, cols), 0) // HD
    c = lax.broadcasted_iota(jnp.int32, (rows, cols), 1) // HD
    return r == c


def compact(full):
    lane = lax.broadcasted_iota(jnp.int32, (HD, full.shape[1]), 1) // HD
    out = jnp.zeros((HD, full.shape[1]), F32)
    for h in range(HEADS):
        out = out + jnp.where(lane == h, full[h * HD : (h + 1) * HD, :], 0.0)
    return out


def block_diag(small):
    width = small.shape[1]
    return jnp.where(same_head(width, width), jnp.concatenate([small] * HEADS, 0), 0.0)


def state_store(st_ref, small, row):
    for s in range(4):
        st_ref[s] = small[8 * s : 8 * s + 8]
    st_ref[4] = jnp.broadcast_to(row, (8, row.shape[1]))
    for s in range(5, 8):
        st_ref[s] = jnp.zeros((8, row.shape[1]), F32)


def state_load(st_ref):
    small = jnp.concatenate([st_ref[s] for s in range(4)], 0)
    return small, st_ref[4][0:1]


def place(zn):
    d, f = lax.axis_index("dom"), lax.axis_index("feat")
    return d, f, d // zn, d % zn, f // CORES, f % CORES


def greet(peers):
    barrier = pltpu.get_barrier_semaphore()
    for peer in peers:
        pl.semaphore_signal(barrier, inc=1, device_id=peer, device_id_type=MESH)
    pl.semaphore_wait(barrier, len(peers))


def send(src, dst, ssem, rsem, dev):
    copy = pltpu.make_async_remote_copy(
        src_ref=src, dst_ref=dst, send_sem=ssem, recv_sem=rsem, device_id=dev, device_id_type=MESH
    )
    copy.start()
    return copy


def ring_peers(xn, zn, yn):
    d, f, x, z, y, c = place(zn)
    feat = [(d, (f + k) % (yn * CORES)) for k in range(1, yn * CORES)]
    zs = [(x * zn + (z + k) % zn, f) for k in range(1, zn)]
    xs = [((x + k) % xn * zn + z, f) for k in range(1, xn)]
    return feat, zs, xs


class Exchange:
    def __init__(self, xn, zn, yn, split_z, src, out, fbuf, zin, zbuf, xbuf, ssem, rsem):
        self.split_z = split_z
        self.src, self.out, self.fbuf, self.zin, self.zbuf, self.xbuf = src, out, fbuf, zin, zbuf, xbuf
        self.ssem, self.rsem = ssem, rsem
        self.used = 0
        self.sent = []
        self.pending = []
        self.xn, self.zn = xn, zn
        self.d, self.f, self.x, self.z, self.y, self.c = place(zn)
        self.feat, self.zs, self.xs = ring_peers(xn, zn, yn)

    def spread(self, srcs, dst, peers):
        copies = []
        for src, peer in zip(srcs, peers):
            n = self.used
            self.used += 1
            copies.append(send(src, dst, self.ssem.at[n], self.rsem.at[n], peer))
        self.sent += copies
        self.pending = copies

    def arrive(self):
        for copy in self.pending:
            copy.wait_recv()
        self.pending = []

    def total(self, buf):
        self.arrive()
        value = buf[0].astype(F32)
        for i in range(1, buf.shape[0]):
            value = value + buf[i].astype(F32)
        return value

    def scatter(self):
        n = len(self.feat) + 1
        self.spread([self.src.at[(self.f + k) % n] for k in range(1, n)], self.fbuf.at[self.f], self.feat)
        self.fbuf[self.f] = self.src[self.f]

    def along_z(self):
        value = self.total(self.fbuf)
        zn, z = self.zn, self.z
        if self.split_z:
            self.zin[...] = value.reshape(self.zin.shape)
            self.zbuf[z] = self.zin[z]
            self.spread([self.zin.at[(z + k) % zn] for k in range(1, zn)], self.zbuf.at[z], self.zs)
        else:
            self.zbuf[z] = value
            self.spread([self.zbuf.at[z]] * len(self.zs), self.zbuf.at[z], self.zs)

    def along_x(self):
        self.xbuf[self.x] = self.total(self.zbuf)
        here = self.xbuf.at[self.x]
        self.spread([here] * len(self.xs), here, self.xs)

    def back_z(self):
        if self.split_z:
            self.zin_out[self.z] = self.total(self.xbuf)
            here = self.zin_out.at[self.z]
            self.spread([here] * len(self.zs), here, self.zs)

    def gather(self):
        if self.split_z:
            self.arrive()
            value = self.zin_out[...].reshape(self.out.shape[1:])
        else:
            value = self.total(self.xbuf)
        self.out[self.f] = value.astype(self.out.dtype)
        here = self.out.at[self.f]
        self.spread([here] * len(self.feat), here, self.feat)

    def finish(self):
        for copy in self.sent:
            copy.wait_send()


def links(xn, zn, yn):
    return 2 * (yn * CORES - 1) + 2 * (zn - 1) + xn - 1


def state_scratch(name, xn, zn, yn, w):
    count = links(xn, zn, yn)
    return [
        (name + "src", pltpu.VMEM((8, 8, w), F32)),
        (name + "f", pltpu.VMEM((8, 8, w), F32)),
        (name + "z", pltpu.VMEM((zn, 8, w), F32)),
        (name + "x", pltpu.VMEM((xn, 8, w), F32)),
        (name + "ss", pltpu.SemaphoreType.DMA((count,))),
        (name + "rs", pltpu.SemaphoreType.DMA((count,))),
    ]


def grad_scratch(name, xn, zn, yn, rows, w):
    count = links(xn, zn, yn)
    n = yn * CORES
    part = rows // n
    return [
        (name + "src", pltpu.VMEM((n, part, w), BF16)),
        (name + "f", pltpu.VMEM((n, part, w), BF16)),
        (name + "zi", pltpu.VMEM((zn, part // zn, w), F32)),
        (name + "zo", pltpu.VMEM((zn, part // zn, w), F32)),
        (name + "z", pltpu.VMEM((zn, part // zn, w), F32)),
        (name + "x", pltpu.VMEM((xn, part // zn, w), F32)),
        (name + "ss", pltpu.SemaphoreType.DMA((count,))),
        (name + "rs", pltpu.SemaphoreType.DMA((count,))),
    ]


def state_sum(name, xn, zn, yn, m, out):
    g = vars(m)
    return Exchange(
        xn, zn, yn, False, g[name + "src"], out, g[name + "f"], None, g[name + "z"], g[name + "x"],
        g[name + "ss"], g[name + "rs"],
    )


def grad_sum(name, xn, zn, yn, m, out):
    g = vars(m)
    red = Exchange(
        xn, zn, yn, True, g[name + "src"], out, g[name + "f"], g[name + "zi"], g[name + "z"], g[name + "x"],
        g[name + "ss"], g[name + "rs"],
    )
    red.zin_out = g[name + "zo"]
    return red


def put_slices(ref, index, value):
    per = ref.shape[1]
    count = value.shape[0] // per
    for s in range(count):
        ref[index * count + s] = value[s * per : (s + 1) * per].astype(ref.dtype)


def layer_kernel(names, xn, zn, yn, *refs):
    m = SimpleNamespace(**dict(zip(names, refs)))
    d, f, x, z, y, c = place(zn)
    dn = xn * zn
    feat, zs, xs = ring_peers(xn, zn, yn)
    sibling = (d, f + 1 - 2 * c)
    yu, yd, yo = (y + 1) % yn, (y + yn - 1) % yn, (y + 2) % yn
    up_y, down_y = (d, yu * CORES + c), (d, yd * CORES + c)
    above, below = ((d + 1) % dn, f), ((d + dn - 1) % dn, f)
    tiles, size = m.adjv.shape[0], m.adjv.shape[1]
    w = m.x.shape[1]
    blocks = m.x.shape[0] // size
    nown = blocks * yn * CORES
    nb = m.lists.shape[1]
    next_ = nown + 2 * nb
    half = size // 2
    hb = blocks // 2
    keep = pl.ds(pl.multiple_of(half * c, half), half)
    other = pl.ds(pl.multiple_of(half * (1 - c), half), half)
    singles = []

    def go(n, src, dst, dev):
        copy = send(src, dst, m.ss.at[n], m.rs.at[n], dev)
        singles.append(copy)
        return copy

    peers = feat + zs + xs + [above, below]
    barrier = pltpu.get_barrier_semaphore()
    for peer in peers:
        pl.semaphore_signal(barrier, inc=1, device_id=peer, device_id_type=MESH)
    fetch = pltpu.make_async_copy(m.adj, m.adjv, m.ls.at[0])
    fetch.start()

    xv = m.x[...]
    key_proj = dot(xv, m.wk[...])
    kf = feature(key_proj).astype(BF16)
    vf = dot(xv, m.wv[...]).astype(BF16)
    m.kf[...] = kf
    m.vf[...] = vf
    state_store(m.asrc, compact(dot_tn(kf, vf)), jnp.sum(kf.astype(F32), axis=0, keepdims=True))
    xblocks = xv.reshape(blocks, size, w)
    m.xo[pl.ds(f * blocks, blocks)] = xblocks

    pl.semaphore_wait(barrier, len(peers))

    red1 = state_sum("a", xn, zn, yn, m, m.ast)
    red2 = state_sum("b", xn, zn, yn, m, m.st2)
    sum1 = grad_sum("c", xn, zn, yn, m, m.g1)
    sum2 = grad_sum("e", xn, zn, yn, m, m.g2)
    red1.scatter()

    def chunk(yy, h, count=1):
        return m.xo.at[pl.ds((yy * CORES + c) * blocks + h * hb, hb * count)]

    a0 = go(0, chunk(y, 0), chunk(y, 0), up_y)
    b1 = go(1, chunk(y, 1), chunk(y, 1), down_y)
    a1 = go(2, chunk(y, 1), chunk(y, 1), up_y)
    b0 = go(3, chunk(y, 0), chunk(y, 0), down_y)
    s_own = go(4, chunk(y, 0, 2), chunk(y, 0, 2), sibling)

    m.qf[...] = feature(dot(xv, m.wq[...])).astype(BF16)
    zero = jnp.zeros((size, w), BF16)
    for b in range(blocks):
        m.g5[b] = (m.cot[b * size : (b + 1) * size, :].astype(F32) * 0.5).astype(BF16)
    m.g5[blocks] = zero
    tpad = -(-tiles // 8) * 8
    down = lax.broadcasted_iota(jnp.int32, (tpad, 128), 0)
    across = lax.broadcasted_iota(jnp.int32, (tpad, 128), 1)

    def chains(table):
        col = jnp.full((tpad, 128), -1, jnp.int32)
        row = jnp.full((1, 128), -2, jnp.int32)
        for t in range(tiles):
            col = jnp.where(down == t, table[t], col)
            row = jnp.where(across[0:1] == t, table[t], row)
        same = (col == row) & (down < across)
        before = jnp.max(jnp.where(same, down, -1), axis=0, keepdims=True)
        final = jnp.max(jnp.where(col == across, down, -1), axis=0, keepdims=True)
        return [jnp.where(v < 0, tiles, v) for v in (before, final)]

    order = chains(m.cols) + chains(m.rows)
    m.ordv[...] = jnp.concatenate(order + order, 0)
    index = pltpu.make_async_copy(m.ordv, m.ords, m.ls.at[1])
    index.start()
    index.wait()
    fetch.wait()

    m.prod[tiles] = jnp.zeros((size, w), F32)
    step = tiles // 4

    def back_one(t, carry):
        m.prod[t] = dot_tn(m.adjv[t], m.g5[m.rows[t]]) + m.prod[m.ords[0, t]]
        return carry

    def back_tiles(part):
        lax.fori_loop(part * step, (part + 1) * step, back_one, 0, unroll=4)

    back_tiles(0)
    back_tiles(1)
    red1.along_z()
    back_tiles(2)
    back_tiles(3)
    red1.along_x()

    def to_sibling(start, count):
        def one(i, carry):
            m.pext[start + i] = m.prod[m.ords[1, start + i], other].astype(BF16)
            return carry

        lax.fori_loop(0, count, one, 0)

    a0.wait_recv()
    fa = go(5, chunk(yd, 0), chunk(yd, 0), up_y)
    b1.wait_recv()
    fb = go(6, chunk(yu, 1), chunk(yu, 1), down_y)
    to_sibling(nown, 2 * nb)
    sib_rim = go(7, m.pext.at[pl.ds(nown, 2 * nb)], m.sib.at[pl.ds(nown, 2 * nb)], sibling)
    s0 = go(8, chunk(yd, 0), chunk(yd, 0), sibling)
    s1 = go(9, chunk(yu, 1), chunk(yu, 1), sibling)
    to_sibling(0, nown)
    sib_own = go(10, m.pext.at[pl.ds(0, nown)], m.sib.at[pl.ds(0, nown)], sibling)
    red1.gather()

    sib_rim.wait_recv()

    def add_rim(i, carry):
        here = nown + i
        m.rimsum[i] = (m.prod[m.ords[1, here], keep] + m.sib[here].astype(F32)).astype(BF16)
        return carry

    lax.fori_loop(0, 2 * nb, add_rim, 0)
    to_below = go(11, m.rimsum.at[pl.ds(0, nb)], m.back.at[0], below)
    to_above = go(12, m.rimsum.at[pl.ds(nb, nb)], m.back.at[1], above)

    a1.wait_recv()
    s2 = go(13, chunk(yd, 1), chunk(yd, 1), sibling)
    b0.wait_recv()
    s3 = go(14, chunk(yu, 0), chunk(yu, 0), sibling)

    red1.arrive()
    small, ks = state_load(m.ast)
    kv = split(block_diag(small), 3)
    ks_col = jnp.broadcast_to(ks, (128, w)).T
    head = same_head(w, w)
    ks_bd = split(jnp.where(head, jnp.concatenate([ks_col] * (w // 128), 1), 0.0), 3)
    q = m.qf[...]
    rden = 1.0 / dots(dot, [q], ks_bd)
    attn = dots(dot, [q], kv) * rden
    g = m.cot[...].astype(F32) * 0.5
    ones = jnp.where(head, 1.0, 0.0).astype(BF16)
    dden = -dots(dot, split(g * attn, 3), [ones]) * rden
    dstate = compact(dots(dot_tn, [q], split(g * rden, 3)))
    state_store(m.bsrc, dstate, jnp.sum(dden * q.astype(F32), axis=0, keepdims=True))
    red2.scatter()
    m.attn[...] = attn
    dqf = dots(dot_nt, [g.astype(BF16)], kv) * rden + dden * ks
    dq = dqf * slope(dot(m.x[...], m.wq[...]))
    m.dq[...] = dq

    fa.wait_recv()
    s4 = go(15, chunk(yo, 0), chunk(yo, 0), sibling)
    fb.wait_recv()
    s5 = go(16, chunk(yo, 1), chunk(yo, 1), sibling)

    xv = m.x[...]
    put_slices(m.csrc, 0, dots(dot_tn, [xv], split(dq, 2)))
    put_slices(m.csrc, 1, dot_tn(xv, m.kf[...]))
    red2.along_z()

    for copy in (s_own, s0, s1, s2, s3, s4, s5):
        copy.wait_recv()
    for s in range(nb):
        m.picks[0, s] = m.xo[m.lists[1, s], keep]
        m.picks[1, s] = m.xo[m.lists[0, s], keep]
    f_above = go(17, m.picks.at[0], m.xr.at[0, :, keep], above)
    f_below = go(18, m.picks.at[1], m.xr.at[1, :, keep], below)
    sum1.scatter()

    sib_own.wait_recv()
    to_below.wait_recv()
    to_above.wait_recv()

    @pl.when(d == dn - 1)
    def _():
        m.back[0] = jnp.zeros(m.back.shape[1:], BF16)

    @pl.when(d == 0)
    def _():
        m.back[1] = jnp.zeros(m.back.shape[1:], BF16)

    def place_rims(base):
        def one(i, carry):
            b = base + i
            value = m.prod[m.ords[1, b], keep] + m.sib[b].astype(F32)
            for s in range(nb):
                value = value + jnp.where(m.lists[1, s] == b, m.back[0, s].astype(F32), 0.0)
                value = value + jnp.where(m.lists[0, s] == b, m.back[1, s].astype(F32), 0.0)
            m.ysend[b] = value.astype(BF16)
            return carry

        lax.fori_loop(0, blocks, one, 0)

    per = 2 * blocks

    def piece(yy, h):
        return m.ysend.at[pl.ds(yy * per + h * blocks, blocks)]

    place_rims(yo * per)
    y0 = go(19, piece(yo, 0), m.ybuf.at[0], up_y)
    place_rims(yo * per + blocks)
    y1 = go(20, piece(yo, 1), m.ybuf.at[1], down_y)
    red2.along_x()
    place_rims(yu * per + blocks)
    y2 = go(21, piece(yu, 1), m.ybuf.at[2], up_y)
    place_rims(yd * per)
    y3 = go(22, piece(yd, 0), m.ybuf.at[3], down_y)
    place_rims(yu * per)
    place_rims(yd * per + blocks)
    red2.gather()
    sum1.along_z()

    def add_piece(n, base):
        def one(i, carry):
            m.ysum[n, i] = (m.ysend[base + i].astype(F32) + m.ybuf[n, i].astype(F32)).astype(BF16)
            return carry

        lax.fori_loop(0, blocks, one, 0)

    y0.wait_recv()
    add_piece(0, yu * per)
    y4 = go(23, m.ysum.at[0], m.ybuf.at[4], up_y)
    y1.wait_recv()
    add_piece(1, yd * per + blocks)
    y5 = go(24, m.ysum.at[1], m.ybuf.at[5], down_y)
    place_rims(y * per)
    place_rims(y * per + blocks)

    def project(value, start):
        here = pl.ds(start, blocks)
        m.xp[here] = value
        value = dot(value.reshape(blocks * size, w), m.wg[...])
        m.ext[here] = value.astype(BF16).reshape(blocks, size, w)

    def project_own(i, carry):
        project(m.xo[pl.ds(i * blocks, blocks)], i * blocks)
        return carry

    lax.fori_loop(0, nown // blocks, project_own, 0)
    f_above.wait_recv()
    f_below.wait_recv()

    @pl.when(d == 0)
    def _():
        m.xr[0, :, keep] = jnp.zeros((nb, half, w), BF16)

    @pl.when(d == dn - 1)
    def _():
        m.xr[1, :, keep] = jnp.zeros((nb, half, w), BF16)

    s6 = go(25, m.xr.at[0, :, keep], m.xr.at[0, :, keep], sibling)
    s7 = go(26, m.xr.at[1, :, keep], m.xr.at[1, :, keep], sibling)
    sum1.along_x()

    red2.arrive()
    small, dks = state_load(m.st2)
    ds = split(block_diag(small), 2)
    xv = m.x[...]
    dk = (dots(dot_nt, [m.vf[...]], ds) + dks) * slope(dot(xv, m.wk[...]))
    put_slices(m.esrc, 0, dots(dot_tn, [xv], split(dk, 2)))
    m.dk[...] = dk

    s6.wait_recv()
    s7.wait_recv()
    for side in range(2):
        for i in range(nb // blocks):
            project(m.xr[side, i * blocks : (i + 1) * blocks], nown + side * nb + i * blocks)
    m.fprod[tiles] = jnp.zeros((size, w), F32)
    m.xprod[tiles] = jnp.zeros((size, w), F32)

    def fore_one(t, carry):
        tile = m.adjv[t]
        b = m.cols[t]
        before = m.ords[2, t]
        m.fprod[t] = dot(tile, m.ext[b]) + m.fprod[before]
        m.xprod[t] = dot(tile, m.xp[b]) + m.xprod[before]
        return carry

    lax.fori_loop(0, tiles // 2, fore_one, 0, unroll=4)
    sum1.back_z()
    lax.fori_loop(tiles // 2, tiles, fore_one, 0, unroll=4)
    graph = None
    for b in range(blocks):
        here = slice(b * size, (b + 1) * size)
        term = dots(dot_tn, split(m.xprod[m.ords[3, b]], 2), [m.g5[b]])
        graph = term if graph is None else graph + term
    put_slices(m.esrc, 1, graph)
    sum2.scatter()
    sum1.gather()
    for b in range(blocks):
        here = slice(b * size, (b + 1) * size)
        m.layer[here, :] = (0.5 * m.attn[here, :] + 0.5 * m.fprod[m.ords[3, b]]).astype(BF16)

    for copy in (y2, y3, y4, y5):
        copy.wait_recv()

    def last(i, carry):
        base = y * per
        m.res[i] = m.ysend[base + i].astype(F32) + m.ybuf[4, i].astype(F32) + m.ybuf[3, i].astype(F32)
        m.res[blocks + i] = (
            m.ysend[base + blocks + i].astype(F32) + m.ybuf[2, i].astype(F32) + m.ybuf[5, i].astype(F32)
        )
        return carry

    lax.fori_loop(0, blocks, last, 0)
    pg_copy = go(27, m.res.at[pl.ds(blocks * (1 - c), blocks)], m.pg.at[:, keep], sibling)
    m.pg[:, keep] = m.res[pl.ds(blocks * c, blocks)]
    sum2.along_z()
    dv = dots(dot, [m.kf[...]], ds)
    total = None
    for grad, weight in ((m.dq[...], m.wq), (m.dk[...], m.wk), (dv, m.wv)):
        term = dots(dot_nt, split(grad, 2), [weight[...]])
        total = term if total is None else total + term
    sum2.along_x()
    pg_copy.wait_recv()
    total = total + dots(dot_nt, split(m.pg[...].reshape(blocks * size, w), 2), [m.wg[...]])
    m.gfeat[...] = total.astype(BF16)
    sum2.back_z()
    sum2.gather()
    sum1.arrive()
    sum2.arrive()
    for red in (red1, red2, sum1, sum2):
        red.finish()
    for copy in singles:
        copy.wait_send()


def last_kernel(layer_i, gfeat_i, c1, c2, st, layer, gfeat, gq, gk, gv, gg):
    layer[...] = layer_i[...]
    gfeat[...] = gfeat_i[...]
    n = gq.shape[0]

    def mat(ref, index):
        per = ref.shape[1]
        count = n // per
        return jnp.concatenate([ref[index * count + s].astype(F32) for s in range(count)], 0)

    gq[...] = mat(c1, 0)
    gk[...] = mat(c2, 0)
    gg[...] = mat(c2, 1)
    small, _ = state_load(st)
    ds = split(block_diag(small), 2)
    gv[...] = dots(dot, split(mat(c1, 1), 2), ds)


def shards(xn, zn, x, wq, wk, wv, wg, adj, rows, cols, lists, cot):
    yn = lax.axis_size("feat") // CORES
    n, w = x.shape
    tiles, size = adj.shape[0], adj.shape[1]
    blocks = n // size
    nown = blocks * yn * CORES
    nb = lists.shape[2]
    next_ = nown + 2 * nb
    lists = lists.reshape(lists.shape[1:])
    S = jax.ShapeDtypeStruct
    V = pltpu.VMEM
    half = size // 2
    part = 2 * w // (yn * CORES)
    singles = 28

    ins = [
        ("rows", SM), ("cols", SM), ("lists", SM), ("x", VM), ("wq", VM), ("wk", VM), ("wv", VM), ("wg", VM),
        ("cot", VM), ("adj", HB),
    ]
    outs = [
        ("layer", S((n, w), BF16)),
        ("gfeat", S((n, w), BF16)),
        ("g1", S((yn * CORES, part, w), BF16)),
        ("g2", S((yn * CORES, part, w), BF16)),
        ("st2", S((8, 8, w), F32)),
    ]
    scratch = [
        ("adjv", V((tiles, size, size), BF16)),
        ("kf", V((n, w), BF16)),
        ("vf", V((n, w), BF16)),
        ("qf", V((n, w), BF16)),
        ("g5", V((blocks + 1, size, w), BF16)),
        ("xo", V((nown, size, w), BF16)),
        ("xr", V((2, nb, size, w), BF16)),
        ("xp", V((next_, size, w), BF16)),
        ("ext", V((next_, size, w), BF16)),
        ("prod", V((tiles + 1, size, w), F32)),
        ("fprod", V((tiles + 1, size, w), F32)),
        ("xprod", V((tiles + 1, size, w), F32)),
        ("pext", V((next_, half, w), BF16)),
        ("sib", V((next_, half, w), BF16)),
        ("rimsum", V((2 * nb, half, w), BF16)),
        ("back", V((2, nb, half, w), BF16)),
        ("picks", V((2, nb, half, w), BF16)),
        ("ysend", V((nown, half, w), BF16)),
        ("ybuf", V((6, blocks, half, w), BF16)),
        ("ysum", V((2, blocks, half, w), BF16)),
        ("res", V((2 * blocks, half, w), F32)),
        ("pg", V((blocks, size, w), F32)),
        ("attn", V((n, w), F32)),
        ("dq", V((n, w), F32)),
        ("dk", V((n, w), F32)),
        ("ast", V((8, 8, w), F32)),
        ("ordv", V((8, 128), jnp.int32)),
        ("ords", pltpu.SMEM((8, 128), jnp.int32)),
        ("ls", pltpu.SemaphoreType.DMA((2,))),
        ("ss", pltpu.SemaphoreType.DMA((singles,))),
        ("rs", pltpu.SemaphoreType.DMA((singles,))),
    ]
    scratch += state_scratch("a", xn, zn, yn, w) + state_scratch("b", xn, zn, yn, w)
    scratch += grad_scratch("c", xn, zn, yn, 2 * w, w) + grad_scratch("e", xn, zn, yn, 2 * w, w)
    names = [name for name, _ in ins + outs + scratch]
    made = pl.pallas_call(
        functools.partial(layer_kernel, names, xn, zn, yn),
        out_shape=[shape for _, shape in outs],
        in_specs=[spec for _, spec in ins],
        out_specs=[VM] * len(outs),
        scratch_shapes=[shape for _, shape in scratch],
        compiler_params=pltpu.CompilerParams(
            collective_id=0, has_side_effects=True, vmem_limit_bytes=LIMIT
        ),
        name="layer",
    )(rows, cols, lists, x, wq, wk, wv, wg, cot, adj)

    return pl.pallas_call(
        last_kernel,
        out_shape=[S((n, w), BF16)] * 2 + [S((w, w), F32)] * 4,
        in_specs=[VM] * 5,
        out_specs=[VM] * 6,
        compiler_params=pltpu.CompilerParams(vmem_limit_bytes=LIMIT),
        name="last",
    )(*made)


def solution(mesh):
    xn, zn = dims(mesh.shape["dom"])
    return jax.shard_map(
        functools.partial(shards, xn, zn),
        mesh=mesh,
        in_specs=(
            P(("dom", "feat"), None),
            P(),
            P(),
            P(),
            P(),
            P(("dom", "feat"), None, None),
            P(("dom", "feat")),
            P(("dom", "feat")),
            P("dom", None, None),
            P(("dom", "feat"), None),
        ),
        out_specs=(P(("dom", "feat"), None), P(("dom", "feat"), None), P(), P(), P(), P()),
        check_vma=False,
    )
```

```python
import functools
from types import SimpleNamespace

import jax
import jax.numpy as jnp
from jax import lax
from jax.experimental import pallas as pl
from jax.experimental.pallas import tpu as pltpu
from jax.sharding import PartitionSpec as P

HEADS = 8
HD = 32
MESH = pl.DeviceIdType.MESH
F32 = jnp.float32
BF16 = jnp.bfloat16
CORES = 2
LIMIT = 56 * 1024 * 1024

VM = pl.BlockSpec(memory_space=pltpu.VMEM)
SM = pl.BlockSpec(memory_space=pltpu.SMEM)
HB = pl.BlockSpec(memory_space=pl.ANY)


def dims(mesh_dom):
    zn = min(8, mesh_dom)
    return mesh_dom // zn, zn


def dot(a, b):
    return jnp.dot(a, b, preferred_element_type=F32)


def dot_tn(a, b):
    return lax.dot_general(a, b, (((0,), (0,)), ((), ())), preferred_element_type=F32)


def dot_nt(a, b):
    return lax.dot_general(a, b, (((1,), (1,)), ((), ())), preferred_element_type=F32)


def split(value, parts):
    out = []
    for _ in range(parts - 1):
        top = value.astype(BF16)
        out.append(top)
        value = value - top.astype(F32)
    out.append(value.astype(BF16))
    return out


def dots(op, a, b):
    terms = [op(p, q) for p in a for q in b]
    total = terms[-1]
    for term in terms[-2::-1]:
        total = total + term
    return total


def feature(z):
    return jnp.where(z > 0, z + 1.0, jnp.exp(jnp.minimum(z, 0.0)))


def slope(z):
    return jnp.where(z > 0, 1.0, jnp.exp(jnp.minimum(z, 0.0)))


def same_head(rows, cols):
    r = lax.broadcasted_iota(jnp.int32, (rows, cols), 0) // HD
    c = lax.broadcasted_iota(jnp.int32, (rows, cols), 1) // HD
    return r == c


def compact(full):
    lane = lax.broadcasted_iota(jnp.int32, (HD, full.shape[1]), 1) // HD
    out = jnp.zeros((HD, full.shape[1]), F32)
    for h in range(HEADS):
        out = out + jnp.where(lane == h, full[h * HD : (h + 1) * HD, :], 0.0)
    return out


def block_diag(small):
    width = small.shape[1]
    return jnp.where(same_head(width, width), jnp.concatenate([small] * HEADS, 0), 0.0)


def state_store(st_ref, small, row):
    for s in range(4):
        st_ref[s] = small[8 * s : 8 * s + 8]
    st_ref[4] = jnp.broadcast_to(row, (8, row.shape[1]))
    for s in range(5, 8):
        st_ref[s] = jnp.zeros((8, row.shape[1]), F32)


def state_load(st_ref):
    small = jnp.concatenate([st_ref[s] for s in range(4)], 0)
    return small, st_ref[4][0:1]


def place(zn):
    d, f = lax.axis_index("dom"), lax.axis_index("feat")
    return d, f, d // zn, d % zn, f // CORES, f % CORES


def greet(peers):
    barrier = pltpu.get_barrier_semaphore()
    for peer in peers:
        pl.semaphore_signal(barrier, inc=1, device_id=peer, device_id_type=MESH)
    pl.semaphore_wait(barrier, len(peers))


def send(src, dst, ssem, rsem, dev):
    copy = pltpu.make_async_remote_copy(
        src_ref=src, dst_ref=dst, send_sem=ssem, recv_sem=rsem, device_id=dev, device_id_type=MESH
    )
    copy.start()
    return copy


def ring_peers(xn, zn, yn):
    d, f, x, z, y, c = place(zn)
    feat = [(d, (f + k) % (yn * CORES)) for k in range(1, yn * CORES)]
    zs = [(x * zn + (z + k) % zn, f) for k in range(1, zn)]
    xs = [((x + k) % xn * zn + z, f) for k in range(1, xn)]
    return feat, zs, xs


class Exchange:
    def __init__(self, group, me, src, out, fbuf, others, ssem, rsem):
        self.group, self.me = group, me
        self.src, self.out, self.fbuf, self.others = src, out, fbuf, others
        self.ssem, self.rsem = ssem, rsem
        self.used = 0
        self.sent = []
        self.pending = []
        self.last = fbuf

    def spread(self, srcs, dst, peers):
        copies = []
        for src, peer in zip(srcs, peers):
            n = self.used
            self.used += 1
            copies.append(send(src, dst, self.ssem.at[n], self.rsem.at[n], peer))
        self.sent += copies
        self.pending = copies

    def arrive(self):
        for copy in self.pending:
            copy.wait_recv()
        self.pending = []

    def total(self):
        self.arrive()
        value = self.last[0].astype(F32)
        for i in range(1, self.last.shape[0]):
            value = value + self.last[i].astype(F32)
        return value

    def scatter(self):
        self.spread([self.src.at[index] for index, _ in self.group], self.fbuf.at[self.me], [p for _, p in self.group])
        self.fbuf[self.me] = self.src[self.me]

    def along(self, n):
        buf, peers, me = self.others[n]
        buf[me] = self.total()
        self.last = buf
        self.spread([buf.at[me]] * len(peers), buf.at[me], peers)

    def gather(self):
        self.out[self.me] = self.total().astype(self.out.dtype)
        here = self.out.at[self.me]
        self.spread([here] * len(self.group), here, [p for _, p in self.group])

    def finish(self):
        for copy in self.sent:
            copy.wait_send()


def plane_group(xn, zn, yn):
    d, f, x, z, y, c = place(zn)
    n = yn * CORES
    group = []
    for i in range(xn):
        for k in range(n):
            if i or k:
                px, pf = (x + i) % xn, (f + k) % n
                group.append((px * n + pf, (px * zn + z, pf)))
    return group, x * n + f


def state_scratch(name, xn, zn, yn, w):
    count = 2 * (yn * CORES - 1) + zn - 1 + xn - 1
    return [
        (name + "src", pltpu.VMEM((8, 8, w), F32)),
        (name + "f", pltpu.VMEM((8, 8, w), F32)),
        (name + "z", pltpu.VMEM((zn, 8, w), F32)),
        (name + "x", pltpu.VMEM((xn, 8, w), F32)),
        (name + "ss", pltpu.SemaphoreType.DMA((count,))),
        (name + "rs", pltpu.SemaphoreType.DMA((count,))),
    ]


def grad_scratch(name, xn, zn, yn, rows, w):
    n = yn * CORES * xn
    count = 2 * (n - 1) + zn - 1
    part = rows // n
    return [
        (name + "src", pltpu.VMEM((n, part, w), BF16)),
        (name + "f", pltpu.VMEM((n, part, w), BF16)),
        (name + "z", pltpu.VMEM((zn, part, w), F32)),
        (name + "ss", pltpu.SemaphoreType.DMA((count,))),
        (name + "rs", pltpu.SemaphoreType.DMA((count,))),
    ]


def state_sum(name, xn, zn, yn, m, out):
    g = vars(m)
    d, f, x, z, y, c = place(zn)
    feat, zs, xs = ring_peers(xn, zn, yn)
    n = len(feat) + 1
    group = [((f + k) % n, feat[k - 1]) for k in range(1, n)]
    others = [(g[name + "z"], zs, z), (g[name + "x"], xs, x)]
    return Exchange(group, f, g[name + "src"], out, g[name + "f"], others, g[name + "ss"], g[name + "rs"])


def grad_sum(name, xn, zn, yn, m, out):
    g = vars(m)
    d, f, x, z, y, c = place(zn)
    _, zs, _ = ring_peers(xn, zn, yn)
    group, me = plane_group(xn, zn, yn)
    others = [(g[name + "z"], zs, z)]
    return Exchange(group, me, g[name + "src"], out, g[name + "f"], others, g[name + "ss"], g[name + "rs"])


def put_slices(ref, index, value):
    per = ref.shape[1]
    count = value.shape[0] // per
    for s in range(count):
        ref[index * count + s] = value[s * per : (s + 1) * per].astype(ref.dtype)


def layer_kernel(names, xn, zn, yn, *refs):
    m = SimpleNamespace(**dict(zip(names, refs)))
    d, f, x, z, y, c = place(zn)
    dn = xn * zn
    feat, zs, xs = ring_peers(xn, zn, yn)
    sibling = (d, f + 1 - 2 * c)
    yu, yd, yo = (y + 1) % yn, (y + yn - 1) % yn, (y + 2) % yn
    up_y, down_y = (d, yu * CORES + c), (d, yd * CORES + c)
    above, below = ((d + 1) % dn, f), ((d + dn - 1) % dn, f)
    tiles, size = m.adjv.shape[0], m.adjv.shape[1]
    w = m.xv.shape[1]
    blocks = m.xv.shape[0] // size
    nown = blocks * yn * CORES
    nb = m.lists.shape[1]
    next_ = nown + 2 * nb
    half = size // 2
    hb = blocks // 2
    keep = pl.ds(pl.multiple_of(half * c, half), half)
    other = pl.ds(pl.multiple_of(half * (1 - c), half), half)
    singles = []

    def go(n, src, dst, dev):
        copy = send(src, dst, m.ss.at[n], m.rs.at[n], dev)
        singles.append(copy)
        return copy

    barrier = pltpu.get_barrier_semaphore()
    plane, _ = plane_group(xn, zn, yn)
    peers = [peer for _, peer in plane] + zs + [above, below]
    for peer in peers:
        pl.semaphore_signal(barrier, inc=1, device_id=peer, device_id_type=MESH)
    inputs = (
        (m.x, m.xv), (m.wk, m.wkv), (m.wv, m.wvv), (m.cot, m.cotv), (m.adj, m.adjv), (m.wq, m.wqv), (m.wg, m.wgv),
    )
    fetch = [pltpu.make_async_copy(a, b, m.ls.at[i]) for i, (a, b) in enumerate(inputs)]
    for copy in fetch:
        copy.start()

    tpad = -(-tiles // 8) * 8
    down = lax.broadcasted_iota(jnp.int32, (tpad, 128), 0)
    across = lax.broadcasted_iota(jnp.int32, (tpad, 128), 1)

    def chains(table):
        col = jnp.full((tpad, 128), -1, jnp.int32)
        row = jnp.full((1, 128), -2, jnp.int32)
        for t in range(tiles):
            col = jnp.where(down == t, table[t], col)
            row = jnp.where(across[0:1] == t, table[t], row)
        same = (col == row) & (down < across)
        before = jnp.max(jnp.where(same, down, -1), axis=0, keepdims=True)
        final = jnp.max(jnp.where(col == across, down, -1), axis=0, keepdims=True)
        return [jnp.where(v < 0, tiles, v) for v in (before, final)]

    order = chains(m.cols) + chains(m.rows)
    m.ordv[...] = jnp.concatenate(order + order, 0)
    index = pltpu.make_async_copy(m.ordv, m.ords, m.ls.at[7])
    index.start()

    for copy in fetch[:3]:
        copy.wait()
    xv = m.xv[...]
    kf = feature(dot(xv, m.wkv[...])).astype(BF16)
    vf = dot(xv, m.wvv[...]).astype(BF16)
    m.kf[...] = kf
    m.vf[...] = vf
    state_store(m.asrc, compact(dot_tn(kf, vf)), jnp.sum(kf.astype(F32), axis=0, keepdims=True))
    m.xo[pl.ds(f * blocks, blocks)] = xv.reshape(blocks, size, w)
    for copy in fetch[3:]:
        copy.wait()
    index.wait()
    for b in range(blocks):
        m.g5[b] = (m.cotv[b * size : (b + 1) * size, :].astype(F32) * 0.5).astype(BF16)
    m.g5[blocks] = jnp.zeros((size, w), BF16)
    m.prod[tiles] = jnp.zeros((size, w), F32)

    red1 = state_sum("a", xn, zn, yn, m, m.ast)
    red2 = state_sum("b", xn, zn, yn, m, m.bst)
    sum1 = grad_sum("c", xn, zn, yn, m, m.cout)
    sum2 = grad_sum("e", xn, zn, yn, m, m.eout)

    pl.semaphore_wait(barrier, len(peers))
    red1.scatter()

    def chunk(yy, h, count=1):
        return m.xo.at[pl.ds((yy * CORES + c) * blocks + h * hb, hb * count)]

    a0 = go(0, chunk(y, 0), chunk(y, 0), up_y)
    b1 = go(1, chunk(y, 1), chunk(y, 1), down_y)
    a1 = go(2, chunk(y, 1), chunk(y, 1), up_y)
    b0 = go(3, chunk(y, 0), chunk(y, 0), down_y)
    s_own = go(4, chunk(y, 0, 2), chunk(y, 0, 2), sibling)

    step = tiles // 2

    def back_one(t, carry):
        m.prod[t] = dot_tn(m.adjv[t], m.g5[m.rows[t]]) + m.prod[m.ords[0, t]]
        return carry

    def back_tiles(part):
        lax.fori_loop(part * step, (part + 1) * step, back_one, 0, unroll=step)

    def to_sibling(start, count):
        def one(i, carry):
            m.pext[start + i] = m.prod[m.ords[1, start + i], other].astype(BF16)
            return carry

        lax.fori_loop(0, count, one, 0)

    back_tiles(0)
    back_tiles(1)
    red1.along(0)
    to_sibling(nown, 2 * nb)
    sib_rim = go(7, m.pext.at[pl.ds(nown, 2 * nb)], m.sib.at[pl.ds(nown, 2 * nb)], sibling)
    a0.wait_recv()
    fa = go(5, chunk(yd, 0), chunk(yd, 0), up_y)
    s0 = go(8, chunk(yd, 0), chunk(yd, 0), sibling)
    b1.wait_recv()
    fb = go(6, chunk(yu, 1), chunk(yu, 1), down_y)
    s1 = go(9, chunk(yu, 1), chunk(yu, 1), sibling)
    to_sibling(0, nown)
    sib_own = go(10, m.pext.at[pl.ds(0, nown)], m.sib.at[pl.ds(0, nown)], sibling)

    sib_rim.wait_recv()

    def add_rim(i, carry):
        here = nown + i
        m.rimsum[i] = (m.prod[m.ords[1, here], keep] + m.sib[here].astype(F32)).astype(BF16)
        return carry

    lax.fori_loop(0, 2 * nb, add_rim, 0)
    to_below = go(11, m.rimsum.at[pl.ds(0, nb)], m.back.at[0], below)
    to_above = go(12, m.rimsum.at[pl.ds(nb, nb)], m.back.at[1], above)

    red1.along(1)
    xv = m.xv[...]
    m.qf[...] = feature(dot(xv, m.wqv[...])).astype(BF16)
    a1.wait_recv()
    s2 = go(13, chunk(yd, 1), chunk(yd, 1), sibling)
    b0.wait_recv()
    s3 = go(14, chunk(yu, 0), chunk(yu, 0), sibling)
    put_slices(m.csrc, 1, dot_tn(xv, m.kf[...]))
    red1.gather()

    fa.wait_recv()
    s4 = go(15, chunk(yo, 0), chunk(yo, 0), sibling)
    fb.wait_recv()
    s5 = go(16, chunk(yo, 1), chunk(yo, 1), sibling)
    for copy in (s_own, s0, s1, s2, s3, s4, s5):
        copy.wait_recv()
    for s in range(nb):
        m.picks[0, s] = m.xo[m.lists[1, s], keep]
        m.picks[1, s] = m.xo[m.lists[0, s], keep]
    f_above = go(17, m.picks.at[0], m.xr.at[0, :, keep], above)
    f_below = go(18, m.picks.at[1], m.xr.at[1, :, keep], below)

    red1.arrive()
    small, ks = state_load(m.ast)
    kv = split(block_diag(small), 3)
    ks_col = jnp.broadcast_to(ks, (128, w)).T
    head = same_head(w, w)
    ks_bd = split(jnp.where(head, jnp.concatenate([ks_col] * (w // 128), 1), 0.0), 3)
    q = m.qf[...]
    rden = 1.0 / dots(dot, [q], ks_bd)
    attn = dots(dot, [q], kv) * rden
    g = m.cotv[...].astype(F32) * 0.5
    ones = jnp.where(head, 1.0, 0.0).astype(BF16)
    dden = -dots(dot, split(g * attn, 3), [ones]) * rden
    dstate = compact(dots(dot_tn, [q], split(g * rden, 3)))
    state_store(m.bsrc, dstate, jnp.sum(dden * q.astype(F32), axis=0, keepdims=True))
    red2.scatter()
    m.attn[...] = attn
    dqf = dots(dot_nt, [g.astype(BF16)], kv) * rden + dden * ks
    xv = m.xv[...]
    dq = dqf * slope(dot(xv, m.wqv[...]))
    m.dq[...] = dq
    put_slices(m.csrc, 0, dots(dot_tn, [xv], split(dq, 2)))

    sib_own.wait_recv()
    to_below.wait_recv()
    to_above.wait_recv()

    @pl.when(d == dn - 1)
    def _():
        m.back[0] = jnp.zeros(m.back.shape[1:], BF16)

    @pl.when(d == 0)
    def _():
        m.back[1] = jnp.zeros(m.back.shape[1:], BF16)

    def place_rims(base):
        def one(i, carry):
            b = base + i
            value = m.prod[m.ords[1, b], keep] + m.sib[b].astype(F32)
            for s in range(nb):
                value = value + jnp.where(m.lists[1, s] == b, m.back[0, s].astype(F32), 0.0)
                value = value + jnp.where(m.lists[0, s] == b, m.back[1, s].astype(F32), 0.0)
            m.ysend[b] = value.astype(BF16)
            return carry

        lax.fori_loop(0, blocks, one, 0)

    per = 2 * blocks

    def piece(yy, h):
        return m.ysend.at[pl.ds(yy * per + h * blocks, blocks)]

    place_rims(yo * per)
    y0 = go(19, piece(yo, 0), m.ybuf.at[0], up_y)
    place_rims(yo * per + blocks)
    y1 = go(20, piece(yo, 1), m.ybuf.at[1], down_y)
    red2.along(0)
    place_rims(yu * per + blocks)
    y2 = go(21, piece(yu, 1), m.ybuf.at[2], up_y)
    place_rims(yd * per)
    y3 = go(22, piece(yd, 0), m.ybuf.at[3], down_y)
    place_rims(yu * per)
    place_rims(yd * per + blocks)

    def project(value, start):
        count = value.shape[0]
        here = pl.ds(start, count)
        m.xp[here] = value
        value = dot(value.reshape(count * size, w), m.wgv[...])
        m.ext[here] = value.astype(BF16).reshape(count, size, w)

    project(m.xo[: nown // 2], 0)
    red2.along(1)
    sum1.scatter()

    def add_piece(n, base):
        def one(i, carry):
            m.ysum[n, i] = (m.ysend[base + i].astype(F32) + m.ybuf[n, i].astype(F32)).astype(BF16)
            return carry

        lax.fori_loop(0, blocks, one, 0)

    red2.gather()
    f_above.wait_recv()
    f_below.wait_recv()

    @pl.when(d == 0)
    def _():
        m.xr[0, :, keep] = jnp.zeros((nb, half, w), BF16)

    @pl.when(d == dn - 1)
    def _():
        m.xr[1, :, keep] = jnp.zeros((nb, half, w), BF16)

    s6 = go(25, m.xr.at[0, :, keep], m.xr.at[0, :, keep], sibling)
    s7 = go(26, m.xr.at[1, :, keep], m.xr.at[1, :, keep], sibling)
    y0.wait_recv()
    add_piece(0, yu * per)
    y4 = go(23, m.ysum.at[0], m.ybuf.at[4], up_y)
    y1.wait_recv()
    add_piece(1, yd * per + blocks)
    y5 = go(24, m.ysum.at[1], m.ybuf.at[5], down_y)
    place_rims(y * per)
    place_rims(y * per + blocks)
    project(m.xo[nown // 2 :], nown // 2)
    s6.wait_recv()
    s7.wait_recv()
    for side in range(2):
        project(m.xr[side], nown + side * nb)
    m.fprod[tiles] = jnp.zeros((size, w), F32)
    m.xprod[tiles] = jnp.zeros((size, w), F32)

    def fore_one(t, carry):
        tile = m.adjv[t]
        b = m.cols[t]
        before = m.ords[2, t]
        m.fprod[t] = dot(tile, m.ext[b]) + m.fprod[before]
        m.xprod[t] = dot(tile, m.xp[b]) + m.xprod[before]
        return carry

    lax.fori_loop(0, tiles, fore_one, 0, unroll=tiles // 2)
    graph = None
    for b in range(blocks):
        term = dots(dot_tn, split(m.xprod[m.ords[3, b]], 2), [m.g5[b]])
        graph = term if graph is None else graph + term
    put_slices(m.esrc, 1, graph)

    red2.arrive()
    small, dks = state_load(m.bst)
    ds = split(block_diag(small), 2)
    xv = m.xv[...]
    dk = (dots(dot_nt, [m.vf[...]], ds) + dks) * slope(dot(xv, m.wkv[...]))
    put_slices(m.esrc, 0, dots(dot_tn, [xv], split(dk, 2)))
    sum2.scatter()
    sum1.along(0)

    for b in range(blocks):
        here = slice(b * size, (b + 1) * size)
        m.layerv[here, :] = (0.5 * m.attn[here, :] + 0.5 * m.fprod[m.ords[3, b]]).astype(BF16)
    outs = [
        pltpu.make_async_copy(m.layerv, m.layer, m.ls.at[8]),
        pltpu.make_async_copy(m.bst, m.st2, m.ls.at[9]),
    ]
    for copy in outs:
        copy.start()
    dv = dots(dot, [m.kf[...]], ds)
    total = None
    for grad, weight in ((m.dq[...], m.wqv), (dk, m.wkv), (dv, m.wvv)):
        term = dots(dot_nt, split(grad, 2), [weight[...]])
        total = term if total is None else total + term

    sum2.along(0)

    for copy in (y2, y3, y4, y5):
        copy.wait_recv()

    def last(i, carry):
        base = y * per
        m.res[i] = m.ysend[base + i].astype(F32) + m.ybuf[4, i].astype(F32) + m.ybuf[3, i].astype(F32)
        m.res[blocks + i] = (
            m.ysend[base + blocks + i].astype(F32) + m.ybuf[2, i].astype(F32) + m.ybuf[5, i].astype(F32)
        )
        return carry

    lax.fori_loop(0, blocks, last, 0)
    pg_copy = go(27, m.res.at[pl.ds(blocks * (1 - c), blocks)], m.pg.at[:, keep], sibling)
    m.pg[:, keep] = m.res[pl.ds(blocks * c, blocks)]
    sum1.gather()
    pg_copy.wait_recv()
    total = total + dots(dot_nt, split(m.pg[...].reshape(blocks * size, w), 2), [m.wgv[...]])
    m.gfeatv[...] = total.astype(BF16)
    outs.append(pltpu.make_async_copy(m.gfeatv, m.gfeat, m.ls.at[10]))
    outs[2].start()
    sum2.gather()
    sum1.arrive()
    outs.append(pltpu.make_async_copy(m.cout, m.g1, m.ls.at[11]))
    outs[3].start()
    sum2.arrive()
    outs.append(pltpu.make_async_copy(m.eout, m.g2, m.ls.at[12]))
    outs[4].start()
    for red in (red1, red2, sum1, sum2):
        red.finish()
    for copy in singles:
        copy.wait_send()
    for copy in outs:
        copy.wait()


def last_kernel(layer_i, gfeat_i, c1, c2, st, layer, gfeat, gq, gk, gv, gg):
    layer[...] = layer_i[...]
    gfeat[...] = gfeat_i[...]
    n = gq.shape[0]

    def mat(ref, index):
        per = ref.shape[1]
        count = n // per
        return jnp.concatenate([ref[index * count + s].astype(F32) for s in range(count)], 0)

    gq[...] = mat(c1, 0)
    gk[...] = mat(c2, 0)
    gg[...] = mat(c2, 1)
    small, _ = state_load(st)
    gv[...] = dots(dot, split(mat(c1, 1), 2), split(block_diag(small), 2))


def shards(xn, zn, x, wq, wk, wv, wg, adj, rows, cols, lists, cot):
    yn = lax.axis_size("feat") // CORES
    n, w = x.shape
    tiles, size = adj.shape[0], adj.shape[1]
    blocks = n // size
    nown = blocks * yn * CORES
    nb = lists.shape[2]
    next_ = nown + 2 * nb
    lists = lists.reshape(lists.shape[1:])
    S = jax.ShapeDtypeStruct
    V = pltpu.VMEM
    half = size // 2
    owners = yn * CORES * xn
    part = 2 * w // owners
    singles = 28

    ins = [
        ("rows", SM), ("cols", SM), ("lists", SM), ("x", HB), ("wq", HB), ("wk", HB), ("wv", HB), ("wg", HB),
        ("cot", HB), ("adj", HB),
    ]
    outs = [
        ("layer", S((n, w), BF16)),
        ("gfeat", S((n, w), BF16)),
        ("g1", S((owners, part, w), BF16)),
        ("g2", S((owners, part, w), BF16)),
        ("st2", S((8, 8, w), F32)),
    ]
    scratch = [
        ("xv", V((n, w), BF16)),
        ("wqv", V((w, w), BF16)),
        ("wkv", V((w, w), BF16)),
        ("wvv", V((w, w), BF16)),
        ("wgv", V((w, w), BF16)),
        ("cotv", V((n, w), BF16)),
        ("adjv", V((tiles, size, size), BF16)),
        ("layerv", V((n, w), BF16)),
        ("gfeatv", V((n, w), BF16)),
        ("cout", V((owners, part, w), BF16)),
        ("eout", V((owners, part, w), BF16)),
        ("bst", V((8, 8, w), F32)),
        ("kf", V((n, w), BF16)),
        ("vf", V((n, w), BF16)),
        ("qf", V((n, w), BF16)),
        ("g5", V((blocks + 1, size, w), BF16)),
        ("xo", V((nown, size, w), BF16)),
        ("xr", V((2, nb, size, w), BF16)),
        ("xp", V((next_, size, w), BF16)),
        ("ext", V((next_, size, w), BF16)),
        ("prod", V((tiles + 1, size, w), F32)),
        ("fprod", V((tiles + 1, size, w), F32)),
        ("xprod", V((tiles + 1, size, w), F32)),
        ("pext", V((next_, half, w), BF16)),
        ("sib", V((next_, half, w), BF16)),
        ("rimsum", V((2 * nb, half, w), BF16)),
        ("back", V((2, nb, half, w), BF16)),
        ("picks", V((2, nb, half, w), BF16)),
        ("ysend", V((nown, half, w), BF16)),
        ("ybuf", V((6, blocks, half, w), BF16)),
        ("ysum", V((2, blocks, half, w), BF16)),
        ("res", V((2 * blocks, half, w), F32)),
        ("pg", V((blocks, size, w), F32)),
        ("attn", V((n, w), F32)),
        ("dq", V((n, w), F32)),
        ("ast", V((8, 8, w), F32)),
        ("ordv", V((8, 128), jnp.int32)),
        ("ords", pltpu.SMEM((8, 128), jnp.int32)),
        ("ls", pltpu.SemaphoreType.DMA((13,))),
        ("ss", pltpu.SemaphoreType.DMA((singles,))),
        ("rs", pltpu.SemaphoreType.DMA((singles,))),
    ]
    scratch += state_scratch("a", xn, zn, yn, w) + state_scratch("b", xn, zn, yn, w)
    scratch += grad_scratch("c", xn, zn, yn, 2 * w, w) + grad_scratch("e", xn, zn, yn, 2 * w, w)
    names = [name for name, _ in ins + outs + scratch]
    made = pl.pallas_call(
        functools.partial(layer_kernel, names, xn, zn, yn),
        out_shape=[shape for _, shape in outs],
        in_specs=[spec for _, spec in ins],
        out_specs=[HB] * len(outs),
        scratch_shapes=[shape for _, shape in scratch],
        compiler_params=pltpu.CompilerParams(
            collective_id=0, has_side_effects=True, vmem_limit_bytes=LIMIT
        ),
        name="layer",
    )(rows, cols, lists, x, wq, wk, wv, wg, cot, adj)

    return pl.pallas_call(
        last_kernel,
        out_shape=[S((n, w), BF16)] * 2 + [S((w, w), F32)] * 4,
        in_specs=[VM] * 5,
        out_specs=[VM] * 6,
        compiler_params=pltpu.CompilerParams(vmem_limit_bytes=LIMIT),
        name="last",
    )(*made)


def solution(mesh):
    xn, zn = dims(mesh.shape["dom"])
    return jax.shard_map(
        functools.partial(shards, xn, zn),
        mesh=mesh,
        in_specs=(
            P(("dom", "feat"), None),
            P(),
            P(),
            P(),
            P(),
            P(("dom", "feat"), None, None),
            P(("dom", "feat")),
            P(("dom", "feat")),
            P("dom", None, None),
            P(("dom", "feat"), None),
        ),
        out_specs=(P(("dom", "feat"), None), P(("dom", "feat"), None), P(), P(), P(), P()),
        check_vma=False,
    )
```

```python
import functools
from types import SimpleNamespace

import jax
import jax.numpy as jnp
from jax import lax
from jax.experimental import pallas as pl
from jax.experimental.pallas import tpu as pltpu
from jax.sharding import PartitionSpec as P

HEADS = 8
HD = 32
MESH = pl.DeviceIdType.MESH
F32 = jnp.float32
BF16 = jnp.bfloat16
CORES = 2
LIMIT = 56 * 1024 * 1024

VM = pl.BlockSpec(memory_space=pltpu.VMEM)
SM = pl.BlockSpec(memory_space=pltpu.SMEM)
HB = pl.BlockSpec(memory_space=pl.ANY)


def dims(mesh_dom):
    zn = min(8, mesh_dom)
    return mesh_dom // zn, zn


def dot(a, b):
    return jnp.dot(a, b, preferred_element_type=F32)


def dot_tn(a, b):
    return lax.dot_general(a, b, (((0,), (0,)), ((), ())), preferred_element_type=F32)


def dot_nt(a, b):
    return lax.dot_general(a, b, (((1,), (1,)), ((), ())), preferred_element_type=F32)


def split(value, parts):
    out = []
    for _ in range(parts - 1):
        top = value.astype(BF16)
        out.append(top)
        value = value - top.astype(F32)
    out.append(value.astype(BF16))
    return out


def dots(op, a, b):
    terms = [op(p, q) for p in a for q in b]
    total = terms[-1]
    for term in terms[-2::-1]:
        total = total + term
    return total


def feature(z):
    return jnp.where(z > 0, z + 1.0, jnp.exp(jnp.minimum(z, 0.0)))


def slope(z):
    return jnp.where(z > 0, 1.0, jnp.exp(jnp.minimum(z, 0.0)))


def same_head(rows, cols):
    r = lax.broadcasted_iota(jnp.int32, (rows, cols), 0) // HD
    c = lax.broadcasted_iota(jnp.int32, (rows, cols), 1) // HD
    return r == c


def compact(full):
    lane = lax.broadcasted_iota(jnp.int32, (HD, full.shape[1]), 1) // HD
    out = jnp.zeros((HD, full.shape[1]), F32)
    for h in range(HEADS):
        out = out + jnp.where(lane == h, full[h * HD : (h + 1) * HD, :], 0.0)
    return out


def block_diag(small):
    width = small.shape[1]
    return jnp.where(same_head(width, width), jnp.concatenate([small] * HEADS, 0), 0.0)


def state_store(st_ref, small, row):
    for s in range(4):
        st_ref[s] = small[8 * s : 8 * s + 8]
    st_ref[4] = jnp.broadcast_to(row, (8, row.shape[1]))
    for s in range(5, 8):
        st_ref[s] = jnp.zeros((8, row.shape[1]), F32)


def state_load(st_ref):
    small = jnp.concatenate([st_ref[s] for s in range(4)], 0)
    return small, st_ref[4][0:1]


def place(zn):
    d, f = lax.axis_index("dom"), lax.axis_index("feat")
    return d, f, d // zn, d % zn, f // CORES, f % CORES


def greet(peers):
    barrier = pltpu.get_barrier_semaphore()
    for peer in peers:
        pl.semaphore_signal(barrier, inc=1, device_id=peer, device_id_type=MESH)
    pl.semaphore_wait(barrier, len(peers))


def send(src, dst, ssem, rsem, dev):
    copy = pltpu.make_async_remote_copy(
        src_ref=src, dst_ref=dst, send_sem=ssem, recv_sem=rsem, device_id=dev, device_id_type=MESH
    )
    copy.start()
    return copy


def ring_peers(xn, zn, yn):
    d, f, x, z, y, c = place(zn)
    feat = [(d, (f + k) % (yn * CORES)) for k in range(1, yn * CORES)]
    zs = [(x * zn + (z + k) % zn, f) for k in range(1, zn)]
    xs = [((x + k) % xn * zn + z, f) for k in range(1, xn)]
    return feat, zs, xs


class Exchange:
    def __init__(self, group, me, src, out, fbuf, others, ssem, rsem, gather=None):
        self.group, self.me = group, me
        self.gather_group, self.gather_me = gather or (group, me)
        self.src, self.out, self.fbuf, self.others = src, out, fbuf, others
        self.ssem, self.rsem = ssem, rsem
        self.used = 0
        self.sent = []
        self.pending = []
        self.last = fbuf

    def spread(self, srcs, dst, peers):
        copies = []
        for src, peer in zip(srcs, peers):
            n = self.used
            self.used += 1
            copies.append(send(src, dst, self.ssem.at[n], self.rsem.at[n], peer))
        self.sent += copies
        self.pending = copies

    def arrive(self):
        for copy in self.pending:
            copy.wait_recv()
        self.pending = []

    def total(self):
        self.arrive()
        value = self.last[0].astype(F32)
        for i in range(1, self.last.shape[0]):
            value = value + self.last[i].astype(F32)
        return value

    def scatter(self):
        self.spread([self.src.at[index] for index, _ in self.group], self.fbuf.at[self.me], [p for _, p in self.group])
        self.fbuf[self.me] = self.src[self.me]

    def along(self, n):
        buf, peers, me = self.others[n]
        buf[me] = self.total()
        self.last = buf
        self.spread([buf.at[me]] * len(peers), buf.at[me], peers)

    def gather(self):
        me, group = self.gather_me, self.gather_group
        self.out[me] = self.total().astype(self.out.dtype)
        here = self.out.at[me]
        self.spread([here] * len(group), here, [p for _, p in group])

    def finish(self):
        for copy in self.sent:
            copy.wait_send()


def plane_group(xn, zn, yn):
    d, f, x, z, y, c = place(zn)
    n = yn * CORES
    group = []
    for i in range(xn):
        for k in range(n):
            if i or k:
                px, pf = (x + i) % xn, (f + k) % n
                group.append((px * n + pf, (px * zn + z, pf)))
    return group, x * n + f


def sum_scratch(name, first, xn, zn, shape, kind, count, third=False):
    out = [
        (name + "src", pltpu.VMEM((first, *shape), kind)),
        (name + "z", pltpu.VMEM((zn, *shape), F32)),
        (name + "ss", pltpu.SemaphoreType.DMA((count,))),
        (name + "rs", pltpu.SemaphoreType.DMA((count,))),
    ]
    if first > 1 or not third:
        out.append((name + "f", pltpu.VMEM((first, *shape), kind)))
    if third:
        out.append((name + "x", pltpu.VMEM((xn, *shape), F32)))
    return out


def make_sums(xn, zn, yn, m):
    d, f, x, z, y, c = place(zn)
    feat, zs, xs = ring_peers(xn, zn, yn)
    n = yn * CORES
    fgroup = [((f + k) % n, feat[k - 1]) for k in range(1, n)]
    xgroup = [((x + k) % xn, xs[k - 1]) for k in range(1, xn)]
    plane, pme = plane_group(xn, zn, yn)
    red1 = Exchange(fgroup, f, m.asrc, m.ast, m.af, [(m.az, zs, z), (m.ax, xs, x)], m.ass, m.ars)
    red2 = Exchange(fgroup, f, None, m.bst, m.bsrc, [(m.bz, zs, z), (m.bx, xs, x)], m.bss, m.brs)
    cots = Exchange(fgroup, f, m.gsrc, None, m.gf, [], m.gss, m.grs)
    sum1 = Exchange(plane, pme, m.csrc, m.cout, m.cf, [(m.cz, zs, z)], m.css, m.crs)
    sum2 = Exchange(plane, pme, m.esrc, m.eout, m.ef, [(m.ez, zs, z)], m.ess, m.ers)
    keys = Exchange(xgroup, x, m.ksrc, m.kout, m.kf_, [(m.kz, zs, z)], m.kss, m.krs, (plane, pme))
    return red1, red2, cots, sum1, sum2, keys


def lanes(rows, cols):
    return (
        lax.broadcasted_iota(jnp.int32, (rows, cols), 0),
        lax.broadcasted_iota(jnp.int32, (rows, cols), 1),
    )


def ones_where(mask):
    return jnp.where(mask, 1.0, 0.0).astype(BF16)


def fold_ones():
    r, c = lanes(128, 128)
    return ones_where(r % HD == c % HD)


def fold_rows(value, groups):
    n = value.shape[0] // groups
    lane = lanes(n, 128)[1] // HD
    out = jnp.zeros((n, 128), F32)
    for q in range(groups):
        out = out + jnp.where(lane == q, value[q * n : (q + 1) * n], 0.0)
    return out


def open_rows(value):
    lane = lanes(value.shape[0], 128)[1] // HD
    return jnp.concatenate([jnp.where(lane == q, value, jnp.zeros((), value.dtype)) for q in range(4)], 0)


def square(rows):
    return jnp.where(same_head(128, 128), jnp.concatenate([rows] * 4, 0), 0.0)


def open_states(ref):
    rows = jnp.concatenate([open_rows(ref[h][0:8]) for h in range(HEADS)], 0)
    rows = dots(dot, split(rows, 3), [fold_ones()])
    width = HEADS * HD
    state = jnp.where(same_head(width, width), jnp.concatenate([rows] * (width // 128), 1), 0.0)
    lane = lanes(1, width)[1] // HD
    ks = jnp.zeros((1, width), F32)
    for h in range(HEADS):
        ks = ks + jnp.where(lane == h, jnp.concatenate([ref[h][8:9]] * (width // 128), 1), 0.0)
    return state, ks


def attention(q, g, state, ks):
    width = ks.shape[1]
    kv = split(state, 3)
    head = same_head(width, width)
    ks_col = jnp.broadcast_to(ks, (128, width)).T
    ks_bd = split(jnp.where(head, jnp.concatenate([ks_col] * (width // 128), 1), 0.0), 3)
    rden = 1.0 / dots(dot, [q], ks_bd)
    attn = dots(dot, [q], kv) * rden
    dden = -dots(dot, split(g * attn, 3), [ones_where(head)]) * rden
    return attn, rden, dden, kv


def put_slices(ref, index, value):
    per = ref.shape[1]
    count = value.shape[0] // per
    for s in range(count):
        ref[index * count + s] = value[s * per : (s + 1) * per].astype(ref.dtype)


def layer_kernel(names, xn, zn, yn, *refs):
    m = SimpleNamespace(**dict(zip(names, refs)))
    d, f, x, z, y, c = place(zn)
    dn = xn * zn
    feat, zs, xs = ring_peers(xn, zn, yn)
    sibling = (d, f + 1 - 2 * c)
    yu, yd, yo = (y + 1) % yn, (y + yn - 1) % yn, (y + 2) % yn
    up_y, down_y = (d, yu * CORES + c), (d, yd * CORES + c)
    above, below = ((d + 1) % dn, f), ((d + dn - 1) % dn, f)
    tiles, size = m.adjv.shape[0], m.adjv.shape[1]
    w = m.xv.shape[1]
    blocks = m.xv.shape[0] // size
    nown = blocks * yn * CORES
    nb = m.lists.shape[1]
    next_ = nown + 2 * nb
    half = size // 2
    hb = blocks // 2
    keep = pl.ds(pl.multiple_of(half * c, half), half)
    other = pl.ds(pl.multiple_of(half * (1 - c), half), half)
    singles = []

    def go(n, src, dst, dev):
        copy = send(src, dst, m.ss.at[n], m.rs.at[n], dev)
        singles.append(copy)
        return copy

    barrier = pltpu.get_barrier_semaphore()
    plane, _ = plane_group(xn, zn, yn)
    peers = [peer for _, peer in plane] + zs + [above, below]
    for peer in peers:
        pl.semaphore_signal(barrier, inc=1, device_id=peer, device_id_type=MESH)
    inputs = (
        (m.x, m.xv), (m.wk, m.wkv), (m.wv, m.wvv), (m.cot, m.cotv), (m.adj, m.adjv), (m.wq, m.wqv), (m.wg, m.wgv),
    )
    fetch = [pltpu.make_async_copy(a, b, m.ls.at[i]) for i, (a, b) in enumerate(inputs)]
    for copy in fetch:
        copy.start()

    tpad = -(-tiles // 8) * 8
    down = lax.broadcasted_iota(jnp.int32, (tpad, 128), 0)
    across = lax.broadcasted_iota(jnp.int32, (tpad, 128), 1)

    def chains(table):
        col = jnp.full((tpad, 128), -1, jnp.int32)
        row = jnp.full((1, 128), -2, jnp.int32)
        for t in range(tiles):
            col = jnp.where(down == t, table[t], col)
            row = jnp.where(across[0:1] == t, table[t], row)
        same = (col == row) & (down < across)
        before = jnp.max(jnp.where(same, down, -1), axis=0, keepdims=True)
        final = jnp.max(jnp.where(col == across, down, -1), axis=0, keepdims=True)
        return [jnp.where(v < 0, tiles, v) for v in (before, final)]

    order = chains(m.cols) + chains(m.rows)
    m.ordv[...] = jnp.concatenate(order + order, 0)
    index = pltpu.make_async_copy(m.ordv, m.ords, m.ls.at[7])
    index.start()

    for copy in fetch[:3]:
        copy.wait()
    xv = m.xv[...]
    kf = feature(dot(xv, m.wkv[...])).astype(BF16)
    vf = dot(xv, m.wvv[...]).astype(BF16)
    m.kf[...] = kf
    m.vf[...] = vf
    ksum = jnp.sum(kf.astype(F32), axis=0, keepdims=True)
    local = jnp.concatenate([compact(dot_tn(kf, vf)), jnp.broadcast_to(ksum, (8, w))], 0)
    er, ec = lanes(w, HEADS * 128)
    pick = (ec // 128 == er // HD) & (ec % HD == er % HD)
    local = dots(dot, split(local, 3), [ones_where(pick)])
    for h in range(HEADS):
        here = local[:, h * 128 : (h + 1) * 128]
        m.asrc[h] = jnp.concatenate([fold_rows(here[:HD], 4), here[HD : HD + 1]], 0)
    m.xo[pl.ds(f * blocks, blocks)] = xv.reshape(blocks, size, w)
    for copy in fetch[3:]:
        copy.wait()
    packed = None
    for b in range(blocks):
        chosen = ones_where(pick & (ec % 128 // HD == b))
        term = dot(m.cotv[b * size : (b + 1) * size, :], chosen)
        packed = term if packed is None else packed + term
    for h in range(HEADS):
        m.gsrc[h] = packed[:, h * 128 : (h + 1) * 128].astype(BF16)
    index.wait()
    for b in range(blocks):
        m.g5[b] = (m.cotv[b * size : (b + 1) * size, :].astype(F32) * 0.5).astype(BF16)
    m.g5[blocks] = jnp.zeros((size, w), BF16)
    m.prod[tiles] = jnp.zeros((size, w), F32)

    red1, red2, cots, sum1, sum2, keys = make_sums(xn, zn, yn, m)

    pl.semaphore_wait(barrier, len(peers))
    red1.scatter()

    def chunk(yy, h, count=1):
        return m.xo.at[pl.ds((yy * CORES + c) * blocks + h * hb, hb * count)]

    a0 = go(0, chunk(y, 0), chunk(y, 0), up_y)
    b1 = go(1, chunk(y, 1), chunk(y, 1), down_y)
    a1 = go(2, chunk(y, 1), chunk(y, 1), up_y)
    b0 = go(3, chunk(y, 0), chunk(y, 0), down_y)
    s_own = go(4, chunk(y, 0, 2), chunk(y, 0, 2), sibling)
    cots.scatter()

    step = tiles // 2

    def back_one(t, carry):
        m.prod[t] = dot_tn(m.adjv[t], m.g5[m.rows[t]]) + m.prod[m.ords[0, t]]
        return carry

    def back_tiles(part):
        lax.fori_loop(part * step, (part + 1) * step, back_one, 0, unroll=step)

    def to_sibling(start, count):
        def one(i, carry):
            m.pext[start + i] = m.prod[m.ords[1, start + i], other].astype(BF16)
            return carry

        lax.fori_loop(0, count, one, 0)

    back_tiles(0)
    back_tiles(1)
    red1.along(0)
    to_sibling(nown, 2 * nb)
    sib_rim = go(7, m.pext.at[pl.ds(nown, 2 * nb)], m.sib.at[pl.ds(nown, 2 * nb)], sibling)
    a0.wait_recv()
    fa = go(5, chunk(yd, 0), chunk(yd, 0), up_y)
    s0 = go(8, chunk(yd, 0), chunk(yd, 0), sibling)
    b1.wait_recv()
    fb = go(6, chunk(yu, 1), chunk(yu, 1), down_y)
    s1 = go(9, chunk(yu, 1), chunk(yu, 1), sibling)
    to_sibling(0, nown)
    sib_own = go(10, m.pext.at[pl.ds(0, nown)], m.sib.at[pl.ds(0, nown)], sibling)

    sib_rim.wait_recv()

    def add_rim(i, carry):
        here = nown + i
        m.rimsum[i] = (m.prod[m.ords[1, here], keep] + m.sib[here].astype(F32)).astype(BF16)
        return carry

    lax.fori_loop(0, 2 * nb, add_rim, 0)
    to_below = go(11, m.rimsum.at[pl.ds(0, nb)], m.back.at[0], below)
    to_above = go(12, m.rimsum.at[pl.ds(nb, nb)], m.back.at[1], above)

    red1.along(1)
    xv = m.xv[...]
    m.qf[...] = feature(dot(xv, m.wqv[...])).astype(BF16)
    a1.wait_recv()
    s2 = go(13, chunk(yd, 1), chunk(yd, 1), sibling)
    b0.wait_recv()
    s3 = go(14, chunk(yu, 0), chunk(yu, 0), sibling)
    put_slices(m.csrc, 1, dot_tn(xv, m.kf[...]))
    red1.gather()

    fa.wait_recv()
    s4 = go(15, chunk(yo, 0), chunk(yo, 0), sibling)
    fb.wait_recv()
    s5 = go(16, chunk(yo, 1), chunk(yo, 1), sibling)
    for copy in (s_own, s0, s1, s2, s3, s4, s5):
        copy.wait_recv()
    for s in range(nb):
        m.picks[0, s] = m.xo[m.lists[1, s], keep]
        m.picks[1, s] = m.xo[m.lists[0, s], keep]
    f_above = go(17, m.picks.at[0], m.xr.at[0, :, keep], above)
    f_below = go(18, m.picks.at[1], m.xr.at[1, :, keep], below)

    count = yn * CORES
    fold = fold_ones()
    hr, hc = lanes(w, 128)
    chosen = [ones_where((hr == f * HD + hc % HD) & (hc // HD == b)) for b in range(blocks)]

    def part_rows(b):
        return jnp.concatenate([m.xo[p * blocks + b] for p in range(count)], 0)

    def by_head(weights):
        total = None
        for b in range(blocks):
            weight = jnp.concatenate([dot(v[...], chosen[b]).astype(BF16) for v in weights], 1)
            term = dot(part_rows(b), weight)
            total = term if total is None else total + term
        return total

    hq = feature(by_head([m.wqv])).astype(BF16)
    cots.arrive()
    hg = m.gf[...].reshape(count * size, 128).astype(F32) * 0.5
    mine = m.ast[f]
    hstate = square(dots(dot, split(open_rows(mine[0:8]), 3), [fold]))
    _, rden, dden, _ = attention(hq, hg, hstate, mine[8:9])
    full = dots(dot_tn, [hq], split(hg * rden, 3))
    group = lanes(HD, 128)[1] // HD
    small = jnp.zeros((HD, 128), F32)
    for b in range(blocks):
        small = small + jnp.where(group == b, full[b * HD : (b + 1) * HD], 0.0)
    dsum = jnp.sum(dden * hq.astype(F32), axis=0, keepdims=True)
    both = jnp.concatenate([small, jnp.broadcast_to(dsum, (8, 128))], 0)
    both = dots(dot, split(both, 3), [fold])
    m.bsrc[0] = jnp.concatenate([fold_rows(both[:HD], 4), both[HD : HD + 1]], 0)
    red2.along(0)
    hkv = by_head([m.wkv, m.wvv])
    m.hkey[...] = hkv[:, :128]
    m.hval[...] = hkv[:, 128:].astype(BF16)

    sib_own.wait_recv()
    to_below.wait_recv()
    to_above.wait_recv()

    @pl.when(d == dn - 1)
    def _():
        m.back[0] = jnp.zeros(m.back.shape[1:], BF16)

    @pl.when(d == 0)
    def _():
        m.back[1] = jnp.zeros(m.back.shape[1:], BF16)

    def place_rims(base):
        def one(i, carry):
            b = base + i
            value = m.prod[m.ords[1, b], keep] + m.sib[b].astype(F32)
            for s in range(nb):
                value = value + jnp.where(m.lists[1, s] == b, m.back[0, s].astype(F32), 0.0)
                value = value + jnp.where(m.lists[0, s] == b, m.back[1, s].astype(F32), 0.0)
            m.ysend[b] = value.astype(BF16)
            return carry

        lax.fori_loop(0, blocks, one, 0)

    per = 2 * blocks

    def piece(yy, h):
        return m.ysend.at[pl.ds(yy * per + h * blocks, blocks)]

    place_rims(yo * per)
    y0 = go(19, piece(yo, 0), m.ybuf.at[0], up_y)
    place_rims(yo * per + blocks)
    y1 = go(20, piece(yo, 1), m.ybuf.at[1], down_y)
    place_rims(yu * per + blocks)
    y2 = go(21, piece(yu, 1), m.ybuf.at[2], up_y)
    place_rims(yd * per)
    y3 = go(22, piece(yd, 0), m.ybuf.at[3], down_y)
    place_rims(yu * per)
    place_rims(yd * per + blocks)

    def project(value, start):
        count = value.shape[0]
        here = pl.ds(start, count)
        m.xp[here] = value
        value = dot(value.reshape(count * size, w), m.wgv[...])
        m.ext[here] = value.astype(BF16).reshape(count, size, w)

    red1.arrive()
    state, ks = open_states(m.ast)
    g = m.cotv[...].astype(F32) * 0.5
    attn, rden, dden, kv = attention(m.qf[...], g, state, ks)
    m.attn[...] = attn
    dqf = dots(dot_nt, [g.astype(BF16)], kv) * rden + dden * ks
    xv = m.xv[...]
    dq = dqf * slope(dot(xv, m.wqv[...]))
    m.dq[...] = dq
    put_slices(m.csrc, 0, dots(dot_tn, [xv], split(dq, 2)))

    sum1.scatter()
    red2.along(1)
    def add_piece(n, base):
        def one(i, carry):
            m.ysum[n, i] = (m.ysend[base + i].astype(F32) + m.ybuf[n, i].astype(F32)).astype(BF16)
            return carry

        lax.fori_loop(0, blocks, one, 0)

    f_above.wait_recv()
    f_below.wait_recv()

    @pl.when(d == 0)
    def _():
        m.xr[0, :, keep] = jnp.zeros((nb, half, w), BF16)

    @pl.when(d == dn - 1)
    def _():
        m.xr[1, :, keep] = jnp.zeros((nb, half, w), BF16)

    s6 = go(25, m.xr.at[0, :, keep], m.xr.at[0, :, keep], sibling)
    s7 = go(26, m.xr.at[1, :, keep], m.xr.at[1, :, keep], sibling)
    project(m.xo[: nown // 2], 0)
    project(m.xo[nown // 2 :], nown // 2)
    s6.wait_recv()
    s7.wait_recv()
    for side in range(2):
        project(m.xr[side], nown + side * nb)
    m.fprod[tiles] = jnp.zeros((size, w), F32)
    m.xprod[tiles] = jnp.zeros((size, w), F32)

    def fore_one(t, carry):
        tile = m.adjv[t]
        b = m.cols[t]
        before = m.ords[2, t]
        m.fprod[t] = dot(tile, m.ext[b]) + m.fprod[before]
        m.xprod[t] = dot(tile, m.xp[b]) + m.xprod[before]
        return carry

    lax.fori_loop(0, tiles, fore_one, 0, unroll=tiles // 2)
    graph = None
    for b in range(blocks):
        term = dots(dot_tn, split(m.xprod[m.ords[3, b]], 2), [m.g5[b]])
        graph = term if graph is None else graph + term
    put_slices(m.esrc, 0, graph)
    sum2.scatter()
    red2.gather()
    mine = m.bst[f]
    hstate = split(square(dots(dot, split(open_rows(mine[0:8]), 3), [fold])), 2)
    hdk = (dots(dot_nt, [m.hval[...]], hstate) + mine[8:9]) * slope(m.hkey[...])
    hdk = split(hdk, 2)
    lane = lanes(w, 128)[1] // HD
    total = jnp.zeros((w, 128), F32)
    for b in range(blocks):
        total = total + jnp.where(lane == b, dots(dot_tn, [part_rows(b)], hdk), 0.0)
    packed = fold_rows(dots(dot, split(total, 3), [fold]), 4)
    m.ksrc[...] = packed.reshape(m.ksrc.shape)
    keys.scatter()
    y0.wait_recv()
    add_piece(0, yu * per)
    y4 = go(23, m.ysum.at[0], m.ybuf.at[4], up_y)
    y1.wait_recv()
    add_piece(1, yd * per + blocks)
    y5 = go(24, m.ysum.at[1], m.ybuf.at[5], down_y)
    place_rims(y * per)
    place_rims(y * per + blocks)
    sum1.along(0)
    keys.along(0)
    red2.arrive()
    state, dks = open_states(m.bst)
    ds = split(state, 2)
    xv = m.xv[...]
    dk = (dots(dot_nt, [m.vf[...]], ds) + dks) * slope(dot(xv, m.wkv[...]))
    for b in range(blocks):
        here = slice(b * size, (b + 1) * size)
        m.layerv[here, :] = (0.5 * m.attn[here, :] + 0.5 * m.fprod[m.ords[3, b]]).astype(BF16)
    outs = [
        pltpu.make_async_copy(m.layerv, m.layer, m.ls.at[8]),
        pltpu.make_async_copy(m.bst, m.st2, m.ls.at[9]),
    ]
    for copy in outs:
        copy.start()
    dv = dots(dot, [m.kf[...]], ds)
    total = None
    for grad, weight in ((m.dq[...], m.wqv), (dk, m.wkv), (dv, m.wvv)):
        term = dots(dot_nt, split(grad, 2), [weight[...]])
        total = term if total is None else total + term

    sum2.along(0)
    keys.gather()
    for copy in (y2, y3, y4, y5):
        copy.wait_recv()

    def last(i, carry):
        base = y * per
        m.res[i] = m.ysend[base + i].astype(F32) + m.ybuf[4, i].astype(F32) + m.ybuf[3, i].astype(F32)
        m.res[blocks + i] = (
            m.ysend[base + blocks + i].astype(F32) + m.ybuf[2, i].astype(F32) + m.ybuf[5, i].astype(F32)
        )
        return carry

    lax.fori_loop(0, blocks, last, 0)
    pg_copy = go(27, m.res.at[pl.ds(blocks * (1 - c), blocks)], m.pg.at[:, keep], sibling)
    m.pg[:, keep] = m.res[pl.ds(blocks * c, blocks)]
    sum1.gather()
    pg_copy.wait_recv()
    total = total + dots(dot_nt, split(m.pg[...].reshape(blocks * size, w), 2), [m.wgv[...]])
    m.gfeatv[...] = total.astype(BF16)
    outs.append(pltpu.make_async_copy(m.gfeatv, m.gfeat, m.ls.at[10]))
    outs[-1].start()
    sum2.gather()
    sum1.arrive()
    keys.arrive()
    outs.append(pltpu.make_async_copy(m.kout, m.g3, m.ls.at[13]))
    outs[-1].start()
    outs.append(pltpu.make_async_copy(m.cout, m.g1, m.ls.at[11]))
    outs[-1].start()
    sum2.arrive()
    outs.append(pltpu.make_async_copy(m.eout, m.g2, m.ls.at[12]))
    outs[-1].start()
    for red in (red1, red2, cots, sum1, sum2, keys):
        red.finish()
    for copy in singles:
        copy.wait_send()
    for copy in outs:
        copy.wait()


def last_kernel(layer_i, gfeat_i, c1, c2, c3, st, layer, gfeat, gq, gk, gv, gg):
    layer[...] = layer_i[...]
    gfeat[...] = gfeat_i[...]
    n = gq.shape[0]

    def mat(ref, index):
        per = ref.shape[1]
        count = n // per
        return jnp.concatenate([ref[index * count + s].astype(F32) for s in range(count)], 0)

    gq[...] = mat(c1, 0)
    gg[...] = mat(c2, 0)
    state, _ = open_states(st)
    gv[...] = dots(dot, split(mat(c1, 1), 2), split(state, 2))
    fold = fold_ones()
    lane = lanes(n, n)[1] // HD
    total = jnp.zeros((n, n), F32)
    for h in range(HEADS):
        rows = jnp.concatenate([c3[p] for p in range(h, c3.shape[0], HEADS)], 0)
        rows = dot(open_rows(rows), fold)
        total = total + jnp.where(lane == h, jnp.concatenate([rows] * (n // 128), 1), 0.0)
    gk[...] = total


def shards(xn, zn, x, wq, wk, wv, wg, adj, rows, cols, lists, cot):
    yn = lax.axis_size("feat") // CORES
    n, w = x.shape
    tiles, size = adj.shape[0], adj.shape[1]
    blocks = n // size
    nown = blocks * yn * CORES
    nb = lists.shape[2]
    next_ = nown + 2 * nb
    lists = lists.reshape(lists.shape[1:])
    S = jax.ShapeDtypeStruct
    V = pltpu.VMEM
    half = size // 2
    owners = yn * CORES * xn
    part = 2 * w // owners
    singles = 28

    ins = [
        ("rows", SM), ("cols", SM), ("lists", SM), ("x", HB), ("wq", HB), ("wk", HB), ("wv", HB), ("wg", HB),
        ("cot", HB), ("adj", HB),
    ]
    outs = [
        ("layer", S((n, w), BF16)),
        ("gfeat", S((n, w), BF16)),
        ("g1", S((owners, part, w), BF16)),
        ("g2", S((owners, part // 2, w), F32)),
        ("g3", S((owners, HD * HEADS // 4 // xn, 128), BF16)),
        ("st2", S((HEADS, 9, 128), F32)),
    ]
    scratch = [
        ("xv", V((n, w), BF16)),
        ("wqv", V((w, w), BF16)),
        ("wkv", V((w, w), BF16)),
        ("wvv", V((w, w), BF16)),
        ("wgv", V((w, w), BF16)),
        ("cotv", V((n, w), BF16)),
        ("adjv", V((tiles, size, size), BF16)),
        ("layerv", V((n, w), BF16)),
        ("gfeatv", V((n, w), BF16)),
        ("cout", V((owners, part, w), BF16)),
        ("eout", V((owners, part // 2, w), F32)),
        ("kout", V((owners, HD * HEADS // 4 // xn, 128), BF16)),
        ("bst", V((HEADS, 9, 128), F32)),
        ("hkey", V((yn * CORES * size, 128), F32)),
        ("hval", V((yn * CORES * size, 128), BF16)),
        ("kf", V((n, w), BF16)),
        ("vf", V((n, w), BF16)),
        ("qf", V((n, w), BF16)),
        ("g5", V((blocks + 1, size, w), BF16)),
        ("xo", V((nown, size, w), BF16)),
        ("xr", V((2, nb, size, w), BF16)),
        ("xp", V((next_, size, w), BF16)),
        ("ext", V((next_, size, w), BF16)),
        ("prod", V((tiles + 1, size, w), F32)),
        ("fprod", V((tiles + 1, size, w), F32)),
        ("xprod", V((tiles + 1, size, w), F32)),
        ("pext", V((next_, half, w), BF16)),
        ("sib", V((next_, half, w), BF16)),
        ("rimsum", V((2 * nb, half, w), BF16)),
        ("back", V((2, nb, half, w), BF16)),
        ("picks", V((2, nb, half, w), BF16)),
        ("ysend", V((nown, half, w), BF16)),
        ("ybuf", V((6, blocks, half, w), BF16)),
        ("ysum", V((2, blocks, half, w), BF16)),
        ("res", V((2 * blocks, half, w), F32)),
        ("pg", V((blocks, size, w), F32)),
        ("attn", V((n, w), F32)),
        ("dq", V((n, w), F32)),
        ("ast", V((HEADS, 9, 128), F32)),
        ("ordv", V((8, 128), jnp.int32)),
        ("ords", pltpu.SMEM((8, 128), jnp.int32)),
        ("ls", pltpu.SemaphoreType.DMA((14,))),
        ("ss", pltpu.SemaphoreType.DMA((singles,))),
        ("rs", pltpu.SemaphoreType.DMA((singles,))),
    ]
    feats, ring, planes = yn * CORES, zn - 1 + xn - 1, owners - 1
    tile = (9, 128)
    scratch += sum_scratch("a", HEADS, xn, zn, tile, F32, 2 * (feats - 1) + ring, third=True)
    scratch += sum_scratch("b", 1, xn, zn, tile, F32, feats - 1 + ring, third=True)
    scratch += sum_scratch("g", HEADS, xn, 1, (size, 128), BF16, feats - 1)
    scratch += sum_scratch("c", owners, xn, zn, (part, w), BF16, 2 * planes + zn - 1)
    scratch += sum_scratch("e", owners, xn, zn, (part // 2, w), F32, 2 * planes + zn - 1)
    scratch += [(n + "_" if n == "kf" else n, v) for n, v in sum_scratch(
        "k", xn, xn, zn, (HD * HEADS // 4 // xn, 128), F32, planes + ring
    )]
    names = [name for name, _ in ins + outs + scratch]
    made = pl.pallas_call(
        functools.partial(layer_kernel, names, xn, zn, yn),
        out_shape=[shape for _, shape in outs],
        in_specs=[spec for _, spec in ins],
        out_specs=[HB] * len(outs),
        scratch_shapes=[shape for _, shape in scratch],
        compiler_params=pltpu.CompilerParams(
            collective_id=0, has_side_effects=True, vmem_limit_bytes=LIMIT
        ),
        name="layer",
    )(rows, cols, lists, x, wq, wk, wv, wg, cot, adj)

    return pl.pallas_call(
        last_kernel,
        out_shape=[S((n, w), BF16)] * 2 + [S((w, w), F32)] * 4,
        in_specs=[VM] * 6,
        out_specs=[VM] * 6,
        compiler_params=pltpu.CompilerParams(vmem_limit_bytes=LIMIT),
        name="last",
    )(*made)


def solution(mesh):
    xn, zn = dims(mesh.shape["dom"])
    return jax.shard_map(
        functools.partial(shards, xn, zn),
        mesh=mesh,
        in_specs=(
            P(("dom", "feat"), None),
            P(),
            P(),
            P(),
            P(),
            P(("dom", "feat"), None, None),
            P(("dom", "feat")),
            P(("dom", "feat")),
            P("dom", None, None),
            P(("dom", "feat"), None),
        ),
        out_specs=(P(("dom", "feat"), None), P(("dom", "feat"), None), P(), P(), P(), P()),
        check_vma=False,
    )
```

```python
import functools
from types import SimpleNamespace

import jax
import jax.numpy as jnp
from jax import lax
from jax.experimental import pallas as pl
from jax.experimental.pallas import tpu as pltpu
from jax.sharding import PartitionSpec as P

HEADS = 8
HD = 32
MESH = pl.DeviceIdType.MESH
F32 = jnp.float32
BF16 = jnp.bfloat16
CORES = 2
LIMIT = 56 * 1024 * 1024

VM = pl.BlockSpec(memory_space=pltpu.VMEM)
SM = pl.BlockSpec(memory_space=pltpu.SMEM)
HB = pl.BlockSpec(memory_space=pl.ANY)


def dims(mesh_dom):
    zn = min(8, mesh_dom)
    return mesh_dom // zn, zn


def dot(a, b):
    return jnp.dot(a, b, preferred_element_type=F32)


def dot_tn(a, b):
    return lax.dot_general(a, b, (((0,), (0,)), ((), ())), preferred_element_type=F32)


def dot_nt(a, b):
    return lax.dot_general(a, b, (((1,), (1,)), ((), ())), preferred_element_type=F32)


def split(value, parts):
    out = []
    for _ in range(parts - 1):
        top = value.astype(BF16)
        out.append(top)
        value = value - top.astype(F32)
    out.append(value.astype(BF16))
    return out


def dots(op, a, b):
    terms = [op(p, q) for p in a for q in b]
    total = terms[-1]
    for term in terms[-2::-1]:
        total = total + term
    return total


def feature(z):
    return jnp.where(z > 0, z + 1.0, jnp.exp(jnp.minimum(z, 0.0)))


def slope(z):
    return jnp.where(z > 0, 1.0, jnp.exp(jnp.minimum(z, 0.0)))


def same_head(rows, cols):
    r = lax.broadcasted_iota(jnp.int32, (rows, cols), 0) // HD
    c = lax.broadcasted_iota(jnp.int32, (rows, cols), 1) // HD
    return r == c


def compact(full):
    lane = lax.broadcasted_iota(jnp.int32, (HD, full.shape[1]), 1) // HD
    out = jnp.zeros((HD, full.shape[1]), F32)
    for h in range(HEADS):
        out = out + jnp.where(lane == h, full[h * HD : (h + 1) * HD, :], 0.0)
    return out


def block_diag(small):
    width = small.shape[1]
    return jnp.where(same_head(width, width), jnp.concatenate([small] * HEADS, 0), 0.0)


def state_store(st_ref, small, row):
    for s in range(4):
        st_ref[s] = small[8 * s : 8 * s + 8]
    st_ref[4] = jnp.broadcast_to(row, (8, row.shape[1]))
    for s in range(5, 8):
        st_ref[s] = jnp.zeros((8, row.shape[1]), F32)


def state_load(st_ref):
    small = jnp.concatenate([st_ref[s] for s in range(4)], 0)
    return small, st_ref[4][0:1]


def place(zn):
    d, f = lax.axis_index("dom"), lax.axis_index("feat")
    return d, f, d // zn, d % zn, f // CORES, f % CORES


def greet(peers):
    barrier = pltpu.get_barrier_semaphore()
    for peer in peers:
        pl.semaphore_signal(barrier, inc=1, device_id=peer, device_id_type=MESH)
    pl.semaphore_wait(barrier, len(peers))


def send(src, dst, ssem, rsem, dev):
    copy = pltpu.make_async_remote_copy(
        src_ref=src, dst_ref=dst, send_sem=ssem, recv_sem=rsem, device_id=dev, device_id_type=MESH
    )
    copy.start()
    return copy


def ring_peers(xn, zn, yn):
    d, f, x, z, y, c = place(zn)
    feat = [(d, (f + k) % (yn * CORES)) for k in range(1, yn * CORES)]
    zs = [(x * zn + (z + k) % zn, f) for k in range(1, zn)]
    xs = [((x + k) % xn * zn + z, f) for k in range(1, xn)]
    return feat, zs, xs


class Exchange:
    def __init__(self, group, me, src, out, fbuf, others, ssem, rsem, gather=None):
        self.group, self.me = group, me
        self.gather_group, self.gather_me = gather or (group, me)
        self.src, self.out, self.fbuf, self.others = src, out, fbuf, others
        self.ssem, self.rsem = ssem, rsem
        self.used = 0
        self.sent = []
        self.pending = []
        self.last = fbuf

    def spread(self, srcs, dst, peers):
        copies = []
        for src, peer in zip(srcs, peers):
            n = self.used
            self.used += 1
            copies.append(send(src, dst, self.ssem.at[n], self.rsem.at[n], peer))
        self.sent += copies
        self.pending = copies

    def arrive(self):
        for copy in self.pending:
            copy.wait_recv()
        self.pending = []

    def total(self):
        self.arrive()
        value = self.last[0].astype(F32)
        for i in range(1, self.last.shape[0]):
            value = value + self.last[i].astype(F32)
        return value

    def scatter(self):
        self.spread([self.src.at[index] for index, _ in self.group], self.fbuf.at[self.me], [p for _, p in self.group])
        self.fbuf[self.me] = self.src[self.me]

    def along(self, n):
        buf, peers, me = self.others[n]
        buf[me] = self.total()
        self.last = buf
        self.spread([buf.at[me]] * len(peers), buf.at[me], peers)

    def gather(self):
        me, group = self.gather_me, self.gather_group
        self.out[me] = self.total().astype(self.out.dtype)
        here = self.out.at[me]
        self.spread([here] * len(group), here, [p for _, p in group])

    def finish(self):
        for copy in self.sent:
            copy.wait_send()


def plane_group(xn, zn, yn):
    d, f, x, z, y, c = place(zn)
    n = yn * CORES
    group = []
    for i in range(xn):
        for k in range(n):
            if i or k:
                px, pf = (x + i) % xn, (f + k) % n
                group.append((px * n + pf, (px * zn + z, pf)))
    return group, x * n + f


def sum_scratch(name, first, xn, zn, shape, kind, count, third=False):
    out = [
        (name + "src", pltpu.VMEM((first, *shape), kind)),
        (name + "z", pltpu.VMEM((zn, *shape), F32)),
        (name + "ss", pltpu.SemaphoreType.DMA((count,))),
        (name + "rs", pltpu.SemaphoreType.DMA((count,))),
    ]
    if first > 1 or not third:
        out.append((name + "f", pltpu.VMEM((first, *shape), kind)))
    if third:
        out.append((name + "x", pltpu.VMEM((xn, *shape), F32)))
    return out


def make_sums(xn, zn, yn, m):
    d, f, x, z, y, c = place(zn)
    feat, zs, xs = ring_peers(xn, zn, yn)
    n = yn * CORES
    fgroup = [((f + k) % n, feat[k - 1]) for k in range(1, n)]
    xgroup = [((x + k) % xn, xs[k - 1]) for k in range(1, xn)]
    plane, pme = plane_group(xn, zn, yn)
    red1 = Exchange(fgroup, f, m.asrc, m.ast, m.af, [(m.az, zs, z), (m.ax, xs, x)], m.ass, m.ars)
    red2 = Exchange(fgroup, f, None, m.bst, m.bsrc, [(m.bz, zs, z), (m.bx, xs, x)], m.bss, m.brs)
    cots = Exchange(fgroup, f, m.gsrc, None, m.gf, [], m.gss, m.grs)
    sum1 = Exchange(plane, pme, m.csrc, m.cout, m.cf, [(m.cz, zs, z)], m.css, m.crs)
    sum2 = Exchange(plane, pme, m.esrc, m.eout, m.ef, [(m.ez, zs, z)], m.ess, m.ers)
    keys = Exchange(xgroup, x, m.ksrc, m.kout, m.kf_, [(m.kz, zs, z)], m.kss, m.krs, (plane, pme))
    return red1, red2, cots, sum1, sum2, keys


def lanes(rows, cols):
    return (
        lax.broadcasted_iota(jnp.int32, (rows, cols), 0),
        lax.broadcasted_iota(jnp.int32, (rows, cols), 1),
    )


def ones_where(mask):
    return jnp.where(mask, 1.0, 0.0).astype(BF16)


def fold_ones():
    r, c = lanes(128, 128)
    return ones_where(r % HD == c % HD)


def fold_rows(value, groups):
    n = value.shape[0] // groups
    lane = lanes(n, 128)[1] // HD
    out = jnp.zeros((n, 128), F32)
    for q in range(groups):
        out = out + jnp.where(lane == q, value[q * n : (q + 1) * n], 0.0)
    return out


def open_rows(value):
    lane = lanes(value.shape[0], 128)[1] // HD
    return jnp.concatenate([jnp.where(lane == q, value, jnp.zeros((), value.dtype)) for q in range(4)], 0)


def square(rows):
    return jnp.where(same_head(128, 128), jnp.concatenate([rows] * 4, 0), 0.0)


def open_states(ref):
    rows = jnp.concatenate([open_rows(ref[h][0:8]) for h in range(HEADS)], 0)
    rows = dots(dot, split(rows, 3), [fold_ones()])
    width = HEADS * HD
    state = jnp.where(same_head(width, width), jnp.concatenate([rows] * (width // 128), 1), 0.0)
    lane = lanes(1, width)[1] // HD
    ks = jnp.zeros((1, width), F32)
    for h in range(HEADS):
        ks = ks + jnp.where(lane == h, jnp.concatenate([ref[h][8:9]] * (width // 128), 1), 0.0)
    return state, ks


def attention(q, g, state, ks):
    width = ks.shape[1]
    kv = split(state, 3)
    head = same_head(width, width)
    ks_col = jnp.broadcast_to(ks, (128, width)).T
    ks_bd = split(jnp.where(head, jnp.concatenate([ks_col] * (width // 128), 1), 0.0), 3)
    rden = 1.0 / dots(dot, [q], ks_bd)
    attn = dots(dot, [q], kv) * rden
    dden = -dots(dot, split(g * attn, 3), [ones_where(head)]) * rden
    return attn, rden, dden, kv


def put_slices(ref, index, value):
    per = ref.shape[1]
    count = value.shape[0] // per
    for s in range(count):
        ref[index * count + s] = value[s * per : (s + 1) * per].astype(ref.dtype)


def layer_kernel(names, xn, zn, yn, *refs):
    m = SimpleNamespace(**dict(zip(names, refs)))
    d, f, x, z, y, c = place(zn)
    dn = xn * zn
    feat, zs, xs = ring_peers(xn, zn, yn)
    sibling = (d, f + 1 - 2 * c)
    yu, yd, yo = (y + 1) % yn, (y + yn - 1) % yn, (y + 2) % yn
    up_y, down_y = (d, yu * CORES + c), (d, yd * CORES + c)
    above, below = ((d + 1) % dn, f), ((d + dn - 1) % dn, f)
    tiles, size = m.adjv.shape[0], m.adjv.shape[1]
    w = m.xv.shape[1]
    blocks = m.xv.shape[0] // size
    nown = blocks * yn * CORES
    nb = m.lists.shape[1]
    next_ = nown + 2 * nb
    half = size // 2
    hb = blocks // 2
    keep = pl.ds(pl.multiple_of(half * c, half), half)
    other = pl.ds(pl.multiple_of(half * (1 - c), half), half)
    singles = []

    def go(n, src, dst, dev):
        copy = send(src, dst, m.ss.at[n], m.rs.at[n], dev)
        singles.append(copy)
        return copy

    barrier = pltpu.get_barrier_semaphore()
    plane, _ = plane_group(xn, zn, yn)
    peers = [peer for _, peer in plane] + zs + [above, below]
    for peer in peers:
        pl.semaphore_signal(barrier, inc=1, device_id=peer, device_id_type=MESH)
    inputs = (
        (m.x, m.xv), (m.wk, m.wkv), (m.wv, m.wvv), (m.cot, m.cotv), (m.adj, m.adjv), (m.wq, m.wqv), (m.wg, m.wgv),
    )
    fetch = [pltpu.make_async_copy(a, b, m.ls.at[i]) for i, (a, b) in enumerate(inputs)]
    for copy in fetch:
        copy.start()

    tpad = -(-tiles // 8) * 8
    down = lax.broadcasted_iota(jnp.int32, (tpad, 128), 0)
    across = lax.broadcasted_iota(jnp.int32, (tpad, 128), 1)

    def chains(table):
        col = jnp.full((tpad, 128), -1, jnp.int32)
        row = jnp.full((1, 128), -2, jnp.int32)
        for t in range(tiles):
            col = jnp.where(down == t, table[t], col)
            row = jnp.where(across[0:1] == t, table[t], row)
        same = (col == row) & (down < across)
        before = jnp.max(jnp.where(same, down, -1), axis=0, keepdims=True)
        final = jnp.max(jnp.where(col == across, down, -1), axis=0, keepdims=True)
        return [jnp.where(v < 0, tiles, v) for v in (before, final)]

    order = chains(m.cols) + chains(m.rows)
    m.ordv[...] = jnp.concatenate(order + order, 0)
    index = pltpu.make_async_copy(m.ordv, m.ords, m.ls.at[7])
    index.start()

    for copy in fetch[:3]:
        copy.wait()
    xv = m.xv[...]
    kf = feature(dot(xv, m.wkv[...])).astype(BF16)
    vf = dot(xv, m.wvv[...]).astype(BF16)
    m.kf[...] = kf
    m.vf[...] = vf
    ksum = jnp.sum(kf.astype(F32), axis=0, keepdims=True)
    local = jnp.concatenate([compact(dot_tn(kf, vf)), jnp.broadcast_to(ksum, (8, w))], 0)
    er, ec = lanes(w, HEADS * 128)
    pick = (ec // 128 == er // HD) & (ec % HD == er % HD)
    local = dots(dot, split(local, 3), [ones_where(pick)])
    for h in range(HEADS):
        here = local[:, h * 128 : (h + 1) * 128]
        m.asrc[h] = jnp.concatenate([fold_rows(here[:HD], 4), here[HD : HD + 1]], 0)
    m.xo[pl.ds(f * blocks, blocks)] = xv.reshape(blocks, size, w)
    for copy in fetch[3:]:
        copy.wait()
    packed = None
    for b in range(blocks):
        chosen = ones_where(pick & (ec % 128 // HD == b))
        term = dot(m.cotv[b * size : (b + 1) * size, :], chosen)
        packed = term if packed is None else packed + term
    for h in range(HEADS):
        m.gsrc[h] = packed[:, h * 128 : (h + 1) * 128].astype(BF16)
    index.wait()
    for b in range(blocks):
        m.g5[b] = (m.cotv[b * size : (b + 1) * size, :].astype(F32) * 0.5).astype(BF16)
    m.g5[blocks] = jnp.zeros((size, w), BF16)
    m.prod[tiles] = jnp.zeros((size, w), F32)

    red1, red2, cots, sum1, sum2, keys = make_sums(xn, zn, yn, m)

    pl.semaphore_wait(barrier, len(peers))
    red1.scatter()

    def chunk(yy, h, count=1):
        return m.xo.at[pl.ds((yy * CORES + c) * blocks + h * hb, hb * count)]

    a0 = go(0, chunk(y, 0), chunk(y, 0), up_y)
    b1 = go(1, chunk(y, 1), chunk(y, 1), down_y)
    a1 = go(2, chunk(y, 1), chunk(y, 1), up_y)
    b0 = go(3, chunk(y, 0), chunk(y, 0), down_y)
    s_own = go(4, chunk(y, 0, 2), chunk(y, 0, 2), sibling)
    cots.scatter()

    step = tiles // 2

    def back_one(t, carry):
        m.prod[t] = dot_tn(m.adjv[t], m.g5[m.rows[t]]) + m.prod[m.ords[0, t]]
        return carry

    def back_tiles(part):
        lax.fori_loop(part * step, (part + 1) * step, back_one, 0, unroll=step)

    def to_sibling(start, count):
        def one(i, carry):
            m.pext[start + i] = m.prod[m.ords[1, start + i], other].astype(BF16)
            return carry

        lax.fori_loop(0, count, one, 0)

    back_tiles(0)
    back_tiles(1)
    red1.along(0)
    to_sibling(nown, 2 * nb)
    sib_rim = go(7, m.pext.at[pl.ds(nown, 2 * nb)], m.sib.at[pl.ds(nown, 2 * nb)], sibling)
    a0.wait_recv()
    fa = go(5, chunk(yd, 0), chunk(yd, 0), up_y)
    s0 = go(8, chunk(yd, 0), chunk(yd, 0), sibling)
    b1.wait_recv()
    fb = go(6, chunk(yu, 1), chunk(yu, 1), down_y)
    s1 = go(9, chunk(yu, 1), chunk(yu, 1), sibling)
    to_sibling(0, nown)
    sib_own = go(10, m.pext.at[pl.ds(0, nown)], m.sib.at[pl.ds(0, nown)], sibling)

    sib_rim.wait_recv()

    def add_rim(i, carry):
        here = nown + i
        m.rimsum[i] = (m.prod[m.ords[1, here], keep] + m.sib[here].astype(F32)).astype(BF16)
        return carry

    lax.fori_loop(0, 2 * nb, add_rim, 0)
    to_below = go(11, m.rimsum.at[pl.ds(0, nb)], m.back.at[0], below)
    to_above = go(12, m.rimsum.at[pl.ds(nb, nb)], m.back.at[1], above)

    red1.along(1)
    xv = m.xv[...]
    m.qf[...] = feature(dot(xv, m.wqv[...])).astype(BF16)
    a1.wait_recv()
    s2 = go(13, chunk(yd, 1), chunk(yd, 1), sibling)
    b0.wait_recv()
    s3 = go(14, chunk(yu, 0), chunk(yu, 0), sibling)
    put_slices(m.csrc, 1, dot_tn(xv, m.kf[...]))
    red1.gather()

    fa.wait_recv()
    s4 = go(15, chunk(yo, 0), chunk(yo, 0), sibling)
    fb.wait_recv()
    s5 = go(16, chunk(yo, 1), chunk(yo, 1), sibling)
    for copy in (s_own, s0, s1, s2, s3, s4, s5):
        copy.wait_recv()
    for s in range(nb):
        m.picks[0, s] = m.xo[m.lists[1, s], keep]
        m.picks[1, s] = m.xo[m.lists[0, s], keep]
    f_above = go(17, m.picks.at[0], m.xr.at[0, :, keep], above)
    f_below = go(18, m.picks.at[1], m.xr.at[1, :, keep], below)

    count = yn * CORES
    fold = fold_ones()
    hr, hc = lanes(w, 128)
    chosen = [ones_where((hr == f * HD + hc % HD) & (hc // HD == b)) for b in range(blocks)]

    def part_rows(b):
        return jnp.concatenate([m.xo[p * blocks + b] for p in range(count)], 0)

    def by_head(weights):
        total = None
        for b in range(blocks):
            weight = jnp.concatenate([dot(v[...], chosen[b]).astype(BF16) for v in weights], 1)
            term = dot(part_rows(b), weight)
            total = term if total is None else total + term
        return total

    hq = feature(by_head([m.wqv])).astype(BF16)
    cots.arrive()
    hg = m.gf[...].reshape(count * size, 128).astype(F32) * 0.5
    mine = m.ast[f]
    hstate = square(dots(dot, split(open_rows(mine[0:8]), 3), [fold]))
    _, rden, dden, _ = attention(hq, hg, hstate, mine[8:9])
    full = dots(dot_tn, [hq], split(hg * rden, 3))
    group = lanes(HD, 128)[1] // HD
    small = jnp.zeros((HD, 128), F32)
    for b in range(blocks):
        small = small + jnp.where(group == b, full[b * HD : (b + 1) * HD], 0.0)
    dsum = jnp.sum(dden * hq.astype(F32), axis=0, keepdims=True)
    both = jnp.concatenate([small, jnp.broadcast_to(dsum, (8, 128))], 0)
    both = dots(dot, split(both, 3), [fold])
    m.bsrc[0] = jnp.concatenate([fold_rows(both[:HD], 4), both[HD : HD + 1]], 0)
    red2.along(0)
    hkv = by_head([m.wkv, m.wvv])
    m.hkey[...] = hkv[:, :128]
    m.hval[...] = hkv[:, 128:].astype(BF16)

    sib_own.wait_recv()
    to_below.wait_recv()
    to_above.wait_recv()

    @pl.when(d == dn - 1)
    def _():
        m.back[0] = jnp.zeros(m.back.shape[1:], BF16)

    @pl.when(d == 0)
    def _():
        m.back[1] = jnp.zeros(m.back.shape[1:], BF16)

    def place_rims(base):
        def one(i, carry):
            b = base + i
            value = m.prod[m.ords[1, b], keep] + m.sib[b].astype(F32)
            for s in range(nb):
                value = value + jnp.where(m.lists[1, s] == b, m.back[0, s].astype(F32), 0.0)
                value = value + jnp.where(m.lists[0, s] == b, m.back[1, s].astype(F32), 0.0)
            m.ysend[b] = value.astype(BF16)
            return carry

        lax.fori_loop(0, blocks, one, 0)

    per = 2 * blocks

    def piece(yy, h):
        return m.ysend.at[pl.ds(yy * per + h * blocks, blocks)]

    place_rims(yo * per)
    y0 = go(19, piece(yo, 0), m.ybuf.at[0], up_y)
    place_rims(yo * per + blocks)
    y1 = go(20, piece(yo, 1), m.ybuf.at[1], down_y)
    place_rims(yu * per + blocks)
    y2 = go(21, piece(yu, 1), m.ybuf.at[2], up_y)
    place_rims(yd * per)
    y3 = go(22, piece(yd, 0), m.ybuf.at[3], down_y)
    place_rims(yu * per)
    place_rims(yd * per + blocks)

    def project(value, start):
        count = value.shape[0]
        here = pl.ds(start, count)
        m.xp[here] = value
        value = dot(value.reshape(count * size, w), m.wgv[...])
        m.ext[here] = value.astype(BF16).reshape(count, size, w)

    red1.arrive()
    state, ks = open_states(m.ast)
    g = m.cotv[...].astype(F32) * 0.5
    attn, rden, dden, kv = attention(m.qf[...], g, state, ks)
    m.attn[...] = attn
    dqf = dots(dot_nt, [g.astype(BF16)], kv) * rden + dden * ks
    xv = m.xv[...]
    dq = dqf * slope(dot(xv, m.wqv[...]))
    m.dq[...] = dq
    put_slices(m.csrc, 0, dots(dot_tn, [xv], split(dq, 2)))

    sum1.scatter()
    red2.along(1)
    def add_piece(n, base):
        def one(i, carry):
            m.ysum[n, i] = (m.ysend[base + i].astype(F32) + m.ybuf[n, i].astype(F32)).astype(BF16)
            return carry

        lax.fori_loop(0, blocks, one, 0)

    f_above.wait_recv()
    f_below.wait_recv()

    @pl.when(d == 0)
    def _():
        m.xr[0, :, keep] = jnp.zeros((nb, half, w), BF16)

    @pl.when(d == dn - 1)
    def _():
        m.xr[1, :, keep] = jnp.zeros((nb, half, w), BF16)

    s6 = go(25, m.xr.at[0, :, keep], m.xr.at[0, :, keep], sibling)
    s7 = go(26, m.xr.at[1, :, keep], m.xr.at[1, :, keep], sibling)
    project(m.xo[: nown // 2], 0)
    project(m.xo[nown // 2 :], nown // 2)
    s6.wait_recv()
    s7.wait_recv()
    for side in range(2):
        project(m.xr[side], nown + side * nb)
    m.fprod[tiles] = jnp.zeros((size, w), F32)
    m.xprod[tiles] = jnp.zeros((size, w), F32)

    def fore_one(t, carry):
        tile = m.adjv[t]
        b = m.cols[t]
        before = m.ords[2, t]
        m.fprod[t] = dot(tile, m.ext[b]) + m.fprod[before]
        m.xprod[t] = dot(tile, m.xp[b]) + m.xprod[before]
        return carry

    lax.fori_loop(0, tiles, fore_one, 0, unroll=tiles // 2)
    graph = None
    for b in range(blocks):
        term = dots(dot_tn, split(m.xprod[m.ords[3, b]], 2), [m.g5[b]])
        graph = term if graph is None else graph + term
    per2 = m.esrc.shape[1] // 2
    for i in range(w // per2):
        here = graph[i * per2 : (i + 1) * per2]
        m.esrc[i] = jnp.concatenate([here[:, :128], here[:, 128:]], 0).astype(BF16)
    sum2.scatter()
    red2.gather()
    mine = m.bst[f]
    hstate = split(square(dots(dot, split(open_rows(mine[0:8]), 3), [fold])), 2)
    hdk = (dots(dot_nt, [m.hval[...]], hstate) + mine[8:9]) * slope(m.hkey[...])
    hdk = split(hdk, 2)
    lane = lanes(w, 128)[1] // HD
    total = jnp.zeros((w, 128), F32)
    for b in range(blocks):
        total = total + jnp.where(lane == b, dots(dot_tn, [part_rows(b)], hdk), 0.0)
    packed = fold_rows(dots(dot, split(total, 3), [fold]), 4)
    m.ksrc[...] = packed.reshape(m.ksrc.shape)
    keys.scatter()
    y0.wait_recv()
    add_piece(0, yu * per)
    y4 = go(23, m.ysum.at[0], m.ybuf.at[4], up_y)
    y1.wait_recv()
    add_piece(1, yd * per + blocks)
    y5 = go(24, m.ysum.at[1], m.ybuf.at[5], down_y)
    place_rims(y * per)
    place_rims(y * per + blocks)
    sum1.along(0)
    keys.along(0)
    red2.arrive()
    state, dks = open_states(m.bst)
    ds = split(state, 2)
    xv = m.xv[...]
    dk = (dots(dot_nt, [m.vf[...]], ds) + dks) * slope(dot(xv, m.wkv[...]))
    for b in range(blocks):
        here = slice(b * size, (b + 1) * size)
        m.layerv[here, :] = (0.5 * m.attn[here, :] + 0.5 * m.fprod[m.ords[3, b]]).astype(BF16)
    outs = [
        pltpu.make_async_copy(m.layerv, m.layer, m.ls.at[8]),
        pltpu.make_async_copy(m.bst, m.st2, m.ls.at[9]),
    ]
    for copy in outs:
        copy.start()
    dv = dots(dot, [m.kf[...]], ds)
    total = None
    for grad, weight in ((m.dq[...], m.wqv), (dk, m.wkv), (dv, m.wvv)):
        term = dots(dot_nt, split(grad, 2), [weight[...]])
        total = term if total is None else total + term

    sum2.along(0)
    keys.gather()
    for copy in (y2, y3, y4, y5):
        copy.wait_recv()

    def last(i, carry):
        base = y * per
        m.res[i] = m.ysend[base + i].astype(F32) + m.ybuf[4, i].astype(F32) + m.ybuf[3, i].astype(F32)
        m.res[blocks + i] = (
            m.ysend[base + blocks + i].astype(F32) + m.ybuf[2, i].astype(F32) + m.ybuf[5, i].astype(F32)
        )
        return carry

    lax.fori_loop(0, blocks, last, 0)
    pg_copy = go(27, m.res.at[pl.ds(blocks * (1 - c), blocks)], m.pg.at[:, keep], sibling)
    m.pg[:, keep] = m.res[pl.ds(blocks * c, blocks)]
    sum1.gather()
    pg_copy.wait_recv()
    total = total + dots(dot_nt, split(m.pg[...].reshape(blocks * size, w), 2), [m.wgv[...]])
    m.gfeatv[...] = total.astype(BF16)
    outs.append(pltpu.make_async_copy(m.gfeatv, m.gfeat, m.ls.at[10]))
    outs[-1].start()
    sum2.gather()
    sum1.arrive()
    keys.arrive()
    outs.append(pltpu.make_async_copy(m.kout, m.g3, m.ls.at[13]))
    outs[-1].start()
    outs.append(pltpu.make_async_copy(m.cout, m.g1, m.ls.at[11]))
    outs[-1].start()
    sum2.arrive()
    outs.append(pltpu.make_async_copy(m.eout, m.g2, m.ls.at[12]))
    outs[-1].start()
    for red in (red1, red2, cots, sum1, sum2, keys):
        red.finish()
    for copy in singles:
        copy.wait_send()
    for copy in outs:
        copy.wait()


def last_kernel(layer_i, gfeat_i, c1, c2, c3, st, layer, gfeat, gq, gk, gv, gg):
    layer[...] = layer_i[...]
    gfeat[...] = gfeat_i[...]
    n = gq.shape[0]

    def mat(ref, index):
        per = ref.shape[1]
        count = n // per
        return jnp.concatenate([ref[index * count + s].astype(F32) for s in range(count)], 0)

    gq[...] = mat(c1, 0)
    per = c2.shape[1] // 2
    for i in range(n // per):
        here = c2[i].astype(F32)
        gg[i * per : (i + 1) * per, :] = jnp.concatenate([here[:per], here[per:]], 1)
    state, _ = open_states(st)
    gv[...] = dots(dot, split(mat(c1, 1), 2), split(state, 2))
    fold = fold_ones()
    lane = lanes(n, n)[1] // HD
    total = jnp.zeros((n, n), F32)
    for h in range(HEADS):
        rows = jnp.concatenate([c3[p] for p in range(h, c3.shape[0], HEADS)], 0)
        rows = dot(open_rows(rows), fold)
        total = total + jnp.where(lane == h, jnp.concatenate([rows] * (n // 128), 1), 0.0)
    gk[...] = total


def shards(xn, zn, x, wq, wk, wv, wg, adj, rows, cols, lists, cot):
    yn = lax.axis_size("feat") // CORES
    n, w = x.shape
    tiles, size = adj.shape[0], adj.shape[1]
    blocks = n // size
    nown = blocks * yn * CORES
    nb = lists.shape[2]
    next_ = nown + 2 * nb
    lists = lists.reshape(lists.shape[1:])
    S = jax.ShapeDtypeStruct
    V = pltpu.VMEM
    half = size // 2
    owners = yn * CORES * xn
    part = 2 * w // owners
    singles = 28

    ins = [
        ("rows", SM), ("cols", SM), ("lists", SM), ("x", HB), ("wq", HB), ("wk", HB), ("wv", HB), ("wg", HB),
        ("cot", HB), ("adj", HB),
    ]
    outs = [
        ("layer", S((n, w), BF16)),
        ("gfeat", S((n, w), BF16)),
        ("g1", S((owners, part, w), BF16)),
        ("g2", S((owners, part, w // 2), BF16)),
        ("g3", S((owners, HD * HEADS // 4 // xn, 128), BF16)),
        ("st2", S((HEADS, 9, 128), F32)),
    ]
    scratch = [
        ("xv", V((n, w), BF16)),
        ("wqv", V((w, w), BF16)),
        ("wkv", V((w, w), BF16)),
        ("wvv", V((w, w), BF16)),
        ("wgv", V((w, w), BF16)),
        ("cotv", V((n, w), BF16)),
        ("adjv", V((tiles, size, size), BF16)),
        ("layerv", V((n, w), BF16)),
        ("gfeatv", V((n, w), BF16)),
        ("cout", V((owners, part, w), BF16)),
        ("eout", V((owners, part, w // 2), BF16)),
        ("kout", V((owners, HD * HEADS // 4 // xn, 128), BF16)),
        ("bst", V((HEADS, 9, 128), F32)),
        ("hkey", V((yn * CORES * size, 128), F32)),
        ("hval", V((yn * CORES * size, 128), BF16)),
        ("kf", V((n, w), BF16)),
        ("vf", V((n, w), BF16)),
        ("qf", V((n, w), BF16)),
        ("g5", V((blocks + 1, size, w), BF16)),
        ("xo", V((nown, size, w), BF16)),
        ("xr", V((2, nb, size, w), BF16)),
        ("xp", V((next_, size, w), BF16)),
        ("ext", V((next_, size, w), BF16)),
        ("prod", V((tiles + 1, size, w), F32)),
        ("fprod", V((tiles + 1, size, w), F32)),
        ("xprod", V((tiles + 1, size, w), F32)),
        ("pext", V((next_, half, w), BF16)),
        ("sib", V((next_, half, w), BF16)),
        ("rimsum", V((2 * nb, half, w), BF16)),
        ("back", V((2, nb, half, w), BF16)),
        ("picks", V((2, nb, half, w), BF16)),
        ("ysend", V((nown, half, w), BF16)),
        ("ybuf", V((6, blocks, half, w), BF16)),
        ("ysum", V((2, blocks, half, w), BF16)),
        ("res", V((2 * blocks, half, w), F32)),
        ("pg", V((blocks, size, w), F32)),
        ("attn", V((n, w), F32)),
        ("dq", V((n, w), F32)),
        ("ast", V((HEADS, 9, 128), F32)),
        ("ordv", V((8, 128), jnp.int32)),
        ("ords", pltpu.SMEM((8, 128), jnp.int32)),
        ("ls", pltpu.SemaphoreType.DMA((14,))),
        ("ss", pltpu.SemaphoreType.DMA((singles,))),
        ("rs", pltpu.SemaphoreType.DMA((singles,))),
    ]
    feats, ring, planes = yn * CORES, zn - 1 + xn - 1, owners - 1
    tile = (9, 128)
    scratch += sum_scratch("a", HEADS, xn, zn, tile, F32, 2 * (feats - 1) + ring, third=True)
    scratch += sum_scratch("b", 1, xn, zn, tile, F32, feats - 1 + ring, third=True)
    scratch += sum_scratch("g", HEADS, xn, 1, (size, 128), BF16, feats - 1)
    scratch += sum_scratch("c", owners, xn, zn, (part, w), BF16, 2 * planes + zn - 1)
    scratch += sum_scratch("e", owners, xn, zn, (part, w // 2), BF16, 2 * planes + zn - 1)
    scratch += [(n + "_" if n == "kf" else n, v) for n, v in sum_scratch(
        "k", xn, xn, zn, (HD * HEADS // 4 // xn, 128), F32, planes + ring
    )]
    names = [name for name, _ in ins + outs + scratch]
    made = pl.pallas_call(
        functools.partial(layer_kernel, names, xn, zn, yn),
        out_shape=[shape for _, shape in outs],
        in_specs=[spec for _, spec in ins],
        out_specs=[HB] * len(outs),
        scratch_shapes=[shape for _, shape in scratch],
        compiler_params=pltpu.CompilerParams(
            collective_id=0, has_side_effects=True, vmem_limit_bytes=LIMIT
        ),
        name="layer",
    )(rows, cols, lists, x, wq, wk, wv, wg, cot, adj)

    return pl.pallas_call(
        last_kernel,
        out_shape=[S((n, w), BF16)] * 2 + [S((w, w), F32)] * 4,
        in_specs=[VM] * 6,
        out_specs=[VM] * 6,
        compiler_params=pltpu.CompilerParams(vmem_limit_bytes=LIMIT),
        name="last",
    )(*made)


def solution(mesh):
    xn, zn = dims(mesh.shape["dom"])
    return jax.shard_map(
        functools.partial(shards, xn, zn),
        mesh=mesh,
        in_specs=(
            P(("dom", "feat"), None),
            P(),
            P(),
            P(),
            P(),
            P(("dom", "feat"), None, None),
            P(("dom", "feat")),
            P(("dom", "feat")),
            P("dom", None, None),
            P(("dom", "feat"), None),
        ),
        out_specs=(P(("dom", "feat"), None), P(("dom", "feat"), None), P(), P(), P(), P()),
        check_vma=False,
    )
```
